512 devices in a mesh: row: 16 (over x_hi, y, core), col: 32 (over x_lo, z).
Axes of the slice: x: 4 (x_hi: 2, x_lo: 2; x = x_hi * 2 + x_lo), y: 4, z: 16, core: 2. Of those that a mesh axis runs over, the one named last changes fastest.
Arguments:
- positions: float32 [16, 32, 3, 256], P('row', 'col'), may hold values from 0 to 8
- species: int32 [16, 32, 256], P('row', 'col'), may hold values from 0 to 1
- atom_valid: int32 [16, 32, 256], P('row', 'col'), may hold values 0 or 1
- row_count: int32 [16, 32], P('row', 'col'), may hold values from 0 to 1
- col_count: int32 [16, 32], P('row', 'col'), may hold values from 0 to 1
- neighbors: int32 [16, 32, 8, 512], P('row', 'col'), may hold values from 0 to 4607
- basis_rate: float32 [8], replicated, may hold values from 0.005 to 0.1
- radial_weight: bfloat16 [8, 512], replicated, may hold values from -2 to 2
- center_table: bfloat16 [2, 512], replicated, may hold values from -3 to 3
- neighbor_table: bfloat16 [2, 512], replicated, may hold values from -3 to 3
- channel_weight: bfloat16 [512, 64], replicated, may hold values from -0.5 to 0.5
- update_weight: bfloat16 [192, 512], replicated, may hold values from -0.45 to 0.45
- energy_weight: bfloat16 [512], replicated, may hold values from -0.25 to 0.25
Outputs:
- forces: float32 [16, 32, 3, 512], P('row', 'col')
- virial: float32 [16, 32, 9, 512], P('row', 'col')
- energies: float32 [16, 32, 512], P('row', 'col')
The draws below stay inside these ranges and needn't reach their ends.
Inputs may be any that keep to these rules, and one draw needn't show every extreme that they name: `neighbors`: A neighbour slot naming an empty atom slot is padding.
All inputs are finite; a program needn't handle non-finite values. No bound on the sum of `atom_valid` on one device may be relied on, other than what follows from the above.
Results may differ from the reference program's by a relative error of at most 0.015.
Values sent between devices are 32-bit elements; how exact they have to be, the bound alone decides.
A program may use at most 64 MiB of HBM per device.

```python
import math
import jax
import jax.numpy as jnp
from jax import lax

C = 64
LATENT = 512
NRB = 8
NSPEC = 2
K = 8
BA = 128
HAND = 1
SLOTS = 2
ATOMS = 512
N_ROW = 16
N_COL = 32


def draw_update_weight(key, part):
    key = jax.random.fold_in(key, 7)
    key_low, key_high, key_sign = jax.random.split(key, 3)
    lower_rows = jax.random.uniform(key_low, (2 * C, LATENT), jnp.float32, -1.0, 1.0) * math.sqrt(1.0 / C)
    magnitude = jax.random.uniform(key_high, (C, LATENT), jnp.float32, 0.25, 0.45)
    flips = jnp.where(jax.random.bernoulli(key_sign, 0.5, (C, LATENT)), 1.0, -1.0)
    return jnp.concatenate([lower_rows, magnitude * flips], axis=0).astype(jnp.bfloat16)


def set_ends(values, rng, low, high):
    place = [jax.random.randint(jax.random.fold_in(rng, axis), (), 0, length) for axis, length in enumerate(values.shape)]
    longest = values.shape.index(max(values.shape))
    neighbour = place[:longest] + [(place[longest] + 1) % values.shape[longest]] + place[longest + 1:]
    return values.at[tuple(place)].set(low).at[tuple(neighbour)].set(high)


def block_scale(key, extent, shards, low, high):
    loudness, own = 1.0, jax.random.fold_in(key, 6)
    for position, blocks in shards:
        heights = jnp.exp(jax.random.uniform(jax.random.fold_in(own, position), (blocks,), jnp.float32, low / len(shards), high / len(shards)))
        loudness = loudness * jnp.repeat(heights, extent[position] // blocks).reshape([-1 if axis == position else 1 for axis in range(len(extent))])
    return loudness


def noise(own_key, shape, scale, most, kind=jnp.bfloat16):
    drawn = scale * jax.random.normal(own_key, shape, jnp.float32)
    return jnp.clip(drawn, min=-most, max=most).astype(kind)


def setup_inputs(seed: int = 0) -> dict:
    streams_of = jax.random.split(jax.random.key(seed), 14)
    positions = jnp.clip(8.0 * jax.random.uniform(streams_of[0], (N_ROW, N_COL, 3, SLOTS * BA), jnp.float32) ** block_scale(streams_of[0], (N_ROW, N_COL, 3, SLOTS * BA), ((0, 16), (1, 32)), -0.2, 0.2), 0.0, 8.0)
    species = set_ends(jax.random.randint(streams_of[1], (N_ROW, N_COL, SLOTS * BA), 0, NSPEC), jax.random.fold_in(streams_of[1], 1), 0, NSPEC - 1).astype(jnp.int32)
    atom_valid = set_ends((jax.random.randint(streams_of[2], (N_ROW, N_COL, SLOTS * BA), 0, 4) < 3).astype(jnp.int32), jax.random.fold_in(streams_of[2], 1), 0, 1)
    row_count = set_ends(jax.random.randint(streams_of[3], (N_ROW, N_COL), 0, HAND + 1), jax.random.fold_in(streams_of[3], 1), 0, HAND).astype(jnp.int32)
    col_count = set_ends(jax.random.randint(streams_of[4], (N_ROW, N_COL), 0, HAND + 1), jax.random.fold_in(streams_of[4], 1), 0, HAND).astype(jnp.int32)
    neighbors = set_ends(jax.random.randint(streams_of[5], (N_ROW, N_COL, K, ATOMS), 0, 9 * ATOMS), jax.random.fold_in(streams_of[5], 1), 0, (9 * ATOMS) - 1).astype(jnp.int32)
    basis_rate = jnp.clip(jnp.exp(jax.random.uniform(streams_of[6], (NRB,), jnp.float32, math.log(0.005), math.log(0.1))), 0.005, 0.1)
    radial_weight = noise(streams_of[7], (NRB, LATENT), NRB ** -0.5, 2.0)
    center_table = noise(streams_of[8], (NSPEC, LATENT), 0.5, 3.0)
    neighbor_table = noise(streams_of[9], (NSPEC, LATENT), 0.5, 3.0)
    channel_weight = noise(streams_of[10], (LATENT, C), (LATENT // 4) ** -0.5, 0.5)
    update_weight = draw_update_weight(jax.random.fold_in(streams_of[13], 71), 0)
    energy_weight = noise(streams_of[12], (LATENT,), LATENT ** -0.5, 0.25)
    return dict(positions=positions, species=species, atom_valid=atom_valid, row_count=row_count, col_count=col_count, neighbors=neighbors, basis_rate=basis_rate, radial_weight=radial_weight, center_table=center_table, neighbor_table=neighbor_table, channel_weight=channel_weight, update_weight=update_weight, energy_weight=energy_weight)


SLAB_WIDTH = 8.0
CUT_SQUARE = 64.0
HARM_SCALE = 0.25
ROOT_THREE = math.sqrt(3.0)

def atom_energies(relative, centre_code, neighbour_code, basis_rate, radial_weight, center_table, neighbor_table, channel_weight, update_weight, energy_weight):
    squared = lax.optimization_barrier(jnp.sum(relative * relative, axis=0))
    active = jnp.logical_and(centre_code[None, :] > 0.5, neighbour_code > 0.5).astype(jnp.float32)
    cutoff = jnp.maximum(1.0 - squared / CUT_SQUARE, 0.0)
    envelope = cutoff * cutoff * active
    radial_basis = (jnp.exp(-basis_rate[:, None, None] * squared[None]) * envelope[None]).astype(jnp.bfloat16)
    species_ids = jnp.arange(1, center_table.shape[0] + 1).astype(jnp.float32)
    center_hot = (centre_code[None, :] == species_ids[:, None]).astype(jnp.float32)
    neighbour_hot = (neighbour_code[None] == species_ids[:, None, None]).astype(jnp.float32)
    pre_latent = jnp.einsum('rl,rkm->lkm', radial_weight.astype(jnp.float32), radial_basis.astype(jnp.float32))
    pre_latent = pre_latent + jnp.einsum('sl,sm->lm', center_table.astype(jnp.float32), center_hot)[:, None, :]
    pre_latent = pre_latent + jnp.einsum('sl,skm->lkm', neighbor_table.astype(jnp.float32), neighbour_hot)
    latent = jax.nn.silu(pre_latent)
    latent_low = latent.astype(jnp.bfloat16)
    channel_mix = jnp.einsum('lc,lkm->ckm', channel_weight.astype(jnp.float32), latent_low.astype(jnp.float32)) * envelope[None]
    along_x = relative[0] * HARM_SCALE
    along_y = relative[1] * HARM_SCALE
    along_z = relative[2] * HARM_SCALE
    norm_sq = along_x * along_x + along_y * along_y + along_z * along_z
    harmonics = jnp.stack([jnp.ones_like(along_x), along_x, along_y, along_z, ROOT_THREE * along_x * along_y, ROOT_THREE * along_y * along_z, 0.5 * (3.0 * along_z * along_z - norm_sq), ROOT_THREE * along_x * along_z, 0.5 * ROOT_THREE * (along_x * along_x - along_y * along_y)])
    features = channel_mix[:, None] * harmonics[None]
    density = lax.optimization_barrier(jnp.sum(features, axis=2)) / math.sqrt(relative.shape[1])
    products = features * density[:, :, None]
    scalars = jnp.stack([products[:, 0], lax.optimization_barrier(jnp.sum(products[:, 1:4], axis=1)), lax.optimization_barrier(jnp.sum(products[:, 4:9], axis=1))])
    channels = scalars.shape[1]
    scalars_low = scalars.reshape((3 * channels,) + scalars.shape[2:]).astype(jnp.bfloat16)
    update = jax.nn.silu(jnp.einsum('sl,skm->lkm', update_weight.astype(jnp.float32), scalars_low.astype(jnp.float32)))
    latent_next = (latent + update).astype(jnp.bfloat16)
    edge_energy = jnp.einsum('l,lkm->km', energy_weight.astype(jnp.float32), latent_next.astype(jnp.float32)) * envelope
    return lax.optimization_barrier(jnp.sum(edge_energy, axis=0))

def edge_terms(relative, centre_code, neighbour_code, weights):

    def energy_of(rel_in):
        return atom_energies(rel_in, centre_code, neighbour_code, *weights)
    energy, pullback = jax.vjp(energy_of, relative)
    gradient = pullback(jnp.ones_like(energy))[0]
    return (energy, gradient)

def device_terms(layout, extended, neighbour_ids, weights):
    relative = extended[:3][:, neighbour_ids] - layout[:3][:, None, :]
    neighbour_code = extended[3][neighbour_ids]
    energy, gradient = edge_terms(relative, layout[3], neighbour_code, weights)
    outer = (relative[:, None] * gradient[None]).reshape((9,) + gradient.shape[1:])
    centre_vals = jnp.concatenate([lax.optimization_barrier(jnp.sum(gradient, axis=1)), -0.5 * lax.optimization_barrier(jnp.sum(outer, axis=1))], axis=0)
    ghost_vals = jnp.concatenate([-gradient, -0.5 * outer], axis=0)
    ghost_acc = jnp.zeros((12, extended.shape[1]), jnp.float32).at[:, neighbour_ids].add(ghost_vals)
    return (energy, centre_vals, ghost_acc)

def reference(positions, species, atom_valid, row_count, col_count, neighbors, basis_rate, radial_weight, center_table, neighbor_table, channel_weight, update_weight, energy_weight):
    code = (atom_valid * (species + 1)).astype(jnp.float32)
    slots_all = positions.shape[3]
    strip = HAND * BA
    strip_block = (jnp.arange(strip) // BA).astype(jnp.int32)
    row_move = (strip_block[None, None, :] < row_count[:, :, None]).astype(jnp.float32)
    col_move = (strip_block[None, None, :] < col_count[:, :, None]).astype(jnp.float32)
    middle = jnp.zeros((N_ROW, N_COL, slots_all - 2 * strip), jnp.float32)
    leaving = jnp.concatenate([col_move, middle, row_move], axis=2)
    own_kept = jnp.concatenate([positions, (code * (1.0 - leaving))[:, :, None, :]], axis=2)
    row_out = jnp.concatenate([positions[..., slots_all - strip:], (code[..., slots_all - strip:] * row_move)[:, :, None, :]], axis=2)
    col_out = jnp.concatenate([positions[..., :strip], (code[..., :strip] * col_move)[:, :, None, :]], axis=2)
    row_shift = jnp.array([-SLAB_WIDTH, 0.0, 0.0, 0.0], jnp.float32)[:, None]
    col_shift = jnp.array([0.0, -SLAB_WIDTH, 0.0, 0.0], jnp.float32)[:, None]
    row_in = jnp.roll(row_out, 1, axis=0) + row_shift
    col_in = jnp.roll(col_out, 1, axis=1) + col_shift
    layout = jnp.concatenate([row_in, col_in, own_kept], axis=3)
    atoms = layout.shape[3]
    pieces = []
    for row_off in range(3):
        for col_off in range(3):
            offset = jnp.array([(row_off - 1) * SLAB_WIDTH, (col_off - 1) * SLAB_WIDTH, 0.0, 0.0], jnp.float32)[:, None]
            pieces.append(jnp.roll(layout, (1 - row_off, 1 - col_off), axis=(0, 1)) + offset)
    extended = jnp.concatenate(pieces, axis=3)
    weights = (basis_rate, radial_weight, center_table, neighbor_table, channel_weight, update_weight, energy_weight)

    def one_device(items):
        return device_terms(items[0], items[1], items[2], weights)

    def flatten(array):
        return array.reshape((N_ROW * N_COL,) + array.shape[2:])
    energy, centre_vals, ghost_acc = lax.map(one_device, (flatten(layout), flatten(extended), flatten(neighbors)))
    ghost = ghost_acc.reshape(N_ROW, N_COL, 12, 3, 3, atoms)
    totals = centre_vals.reshape(N_ROW, N_COL, 12, atoms)
    for row_off in range(3):
        for col_off in range(3):
            totals = totals + jnp.roll(ghost[:, :, :, row_off, col_off, :], (row_off - 1, col_off - 1), axis=(0, 1))
    return (totals[:, :, :3], totals[:, :, 3:], energy.reshape(N_ROW, N_COL, atoms))
```

```python
import functools
import math

import jax
import jax.numpy as jnp
from jax import lax
from jax.experimental import pallas as pl
from jax.experimental.pallas import tpu as pltpu
from jax.sharding import PartitionSpec as P

K = 8
BA = 128
C = 64
LAT = 512
ATOMS = 512
SPAN = 256
GROUPS = 18
SLAB = 8.0
SCALE = 0.25
ROOT3 = math.sqrt(3.0)
NORM = 1.0 / math.sqrt(8.0)
F32 = jnp.float32
BF16 = jnp.bfloat16
MESH = pl.DeviceIdType.MESH

NEAR = [(a, b) for a in (-1, 0, 1) for b in (-1, 0, 1) if (a, b) != (0, 0)]
REACH = NEAR + [(2, b) for b in (-1, 0, 1)] + [(a, 2) for a in (-1, 0, 1)]
DEGREE = [0, 1, 1, 1, 2, 2, 2, 2, 2]
CHUNK = 128


def dot(a, b):
    return lax.dot_general(a, b, (((1,), (0,)), ((), ())), preferred_element_type=F32)


def dot_nt(a, b):
    return lax.dot_general(a, b, (((1,), (1,)), ((), ())), preferred_element_type=F32)


def kernel(
    n_row,
    n_col,
    pos,
    spc,
    valid,
    rcount,
    ccount,
    nbr,
    rate,
    rw,
    ct,
    nt,
    cw,
    uw,
    ew,
    forces,
    virial,
    energies,
    own,
    inbox,
    near_table,
    rel_code,
    onehot,
    harm,
    edge,
    w_stage,
    w1t,
    w1,
    wut,
    wue,
    wct,
    wcc,
    ew16,
    latent,
    slope1,
    updated,
    slope2,
    mix0,
    mix,
    dens,
    ddens,
    prods,
    scal,
    dscal,
    dmix,
    dharm,
    dlow,
    dpre,
    vals,
    ghost,
    ghost_in,
    send_in,
    recv_in,
    send_out,
    recv_out,
):
    row = lax.axis_index("row")
    col = lax.axis_index("col")

    def at(dr, dc):
        return (lax.rem(row + (dr + n_row), n_row), lax.rem(col + (dc + n_col), n_col))

    barrier = pltpu.get_barrier_semaphore()
    for dr, dc in REACH:
        pl.semaphore_signal(barrier, inc=1, device_id=at(-dr, -dc), device_id_type=MESH)

    code = (valid[0] * (spc[0] + 1)).astype(F32)
    moves = jnp.concatenate(
        [
            jnp.where(jnp.broadcast_to(ccount[...], (1, BA)) > 0, 1.0, 0.0),
            jnp.where(jnp.broadcast_to(rcount[...], (1, BA)) > 0, 1.0, 0.0),
        ],
        axis=1,
    )
    own[...] = jnp.zeros_like(own)
    own[0:3, :] = pos[0, 0]
    own[3:4, :] = code * (1.0 - moves)
    own[4:5, :] = code * moves
    pl.semaphore_wait(barrier, len(REACH))
    sends = []
    for slot, (dr, dc) in enumerate(REACH):
        copy = pltpu.make_async_remote_copy(
            src_ref=own,
            dst_ref=inbox.at[slot],
            send_sem=send_in.at[slot],
            recv_sem=recv_in.at[slot],
            device_id=at(dr, dc),
            device_id_type=MESH,
        )
        copy.start()
        sends.append(copy)

    w_stage[...] = jnp.zeros_like(w_stage)
    w_stage[0:8, :] = rw[...].astype(F32) * 0.5
    w_stage[8:10, :] = ct[...].astype(F32) * 0.5
    w_stage[10:12, :] = nt[...].astype(F32) * 0.5
    w1[...] = w_stage[0:16, :].astype(BF16)
    w1t[...] = w_stage[...].T[:, 0:16].astype(BF16)
    half_u = uw[...].astype(F32) * 0.5
    ew_row = ew[...].astype(F32)
    wue[...] = (half_u * ew_row).astype(BF16)
    wut[...] = half_u.T.astype(BF16)
    w_stage[0:C, :] = cw[...].astype(F32).T
    w_stage[C : C + 1, :] = ew_row
    w_stage[C + 1 : C + 2, :] = ew_row
    wct[...] = w_stage[0:80, :].astype(BF16)
    wcc[...] = w_stage[...].T[:, 0:80].astype(BF16)
    ew16[...] = jnp.broadcast_to(ew_row, (16, LAT)).astype(BF16)

    place_of = lax.broadcasted_iota(jnp.int32, (SPAN, ATOMS), 0)

    def mark(k, carry):
        place = nbr[0, 0, pl.ds(k, 1), :] & (SPAN - 1)
        onehot[k] = jnp.where(place_of == place, 1.0, 0.0).astype(BF16)
        return carry

    lax.fori_loop(0, K, mark, 0)

    for copy in sends:
        copy.wait_recv()

    row_of = lax.broadcasted_iota(jnp.int32, (8, BA), 0)

    def source(dr, dc):
        if (dr, dc) == (0, 0):
            return own
        return inbox.at[REACH.index((-dr, -dc))]

    def offset(x, y):
        return jnp.where(row_of == 0, x, 0.0) + jnp.where(row_of == 1, y, 0.0)

    def moved(block):
        return jnp.where(row_of == 3, pltpu.roll(block, 7, 0), block)

    centre = []
    for a in (-1, 0, 1):
        for b in (-1, 0, 1):
            x, y = SLAB * a, SLAB * b
            base = 16 * ((a + 1) * 3 + b + 1)
            tiles = [
                moved(source(a - 1, b)[:, BA:]) + offset(x - SLAB, y),
                moved(source(a, b - 1)[:, :BA]) + offset(x, y - SLAB),
                source(a, b)[:, :BA] + offset(x, y),
                source(a, b)[:, BA:] + offset(x, y),
            ]
            if (a, b) == (0, 0):
                centre = tiles
            for q, tile in enumerate(tiles):
                high = tile.astype(BF16)
                low = (tile - high.astype(F32)).astype(BF16)
                near_table[0, base + 8 * (q // 2) : base + 8 * (q // 2) + 8, BA * (q % 2) : BA * (q % 2) + BA] = high.astype(F32)
                near_table[1, base + 8 * (q // 2) : base + 8 * (q // 2) + 8, BA * (q % 2) : BA * (q % 2) + BA] = low.astype(F32)
    centre = jnp.concatenate(centre, axis=1)
    centre_xyz = jnp.where(lax.broadcasted_iota(jnp.int32, (8, ATOMS), 0) < 3, centre, 0.0)
    centre_code = centre[3:4, :]

    def gather(k, carry):
        group = jnp.broadcast_to(nbr[0, 0, pl.ds(k, 1), :] // SPAN, (8, ATOMS))
        hot = onehot[k]
        found = dot(near_table[0].astype(BF16), hot) + dot(near_table[1].astype(BF16), hot)
        picked = found[0:8]
        for g in range(1, GROUPS):
            picked = jnp.where(group == g, found[8 * g : 8 * g + 8], picked)
        picked = picked - centre_xyz
        for j in range(ATOMS // BA):
            rel_code[j, pl.ds(pl.multiple_of(8 * k, 8), 8), :] = picked[:, j * BA : j * BA + BA]
        return carry

    lax.fori_loop(0, K, gather, 0)

    rx, ry, rz, ncode = [
        jnp.concatenate([rel_code[j, pl.ds(c, K, stride=8), :] for j in range(ATOMS // BA)], axis=1)
        for c in range(4)
    ]
    live = jnp.where(jnp.logical_and(ncode > 0.5, centre_code > 0.5), 1.0, 0.0)
    sq = rx * rx + ry * ry + rz * rz
    cut = jnp.maximum(1.0 - sq * (1.0 / 64.0), 0.0)
    env = cut * cut * live
    ux, uy, uz = rx * SCALE, ry * SCALE, rz * SCALE
    norm = ux * ux + uy * uy + uz * uz
    for m, h in enumerate(
        [
            ux,
            uy,
            uz,
            ROOT3 * ux * uy,
            ROOT3 * uy * uz,
            0.5 * (3.0 * uz * uz - norm),
            ROOT3 * ux * uz,
            0.5 * ROOT3 * (ux * ux - uy * uy),
        ]
    ):
        harm[m + 1] = h
    edge[0] = sq
    edge[1] = env
    edge[2] = ncode

    row8 = lax.broadcasted_iota(jnp.int32, (8, ATOMS), 0)
    rates = jnp.zeros((8, ATOMS), F32)
    for n in range(8):
        rates = jnp.where(row8 == n, rate[n], rates)
    kind = jnp.where(row8 % 2 == 0, 1.0, 2.0)

    def first(k, carry):
        sq_k = edge[0, pl.ds(k, 1), :]
        env_k = edge[1, pl.ds(k, 1), :]
        basis = jnp.exp(-rates * sq_k) * env_k
        codes = jnp.where(row8 < 2, centre_code, edge[2, pl.ds(k, 1), :])
        hot = jnp.where(jnp.logical_and(codes == kind, row8 < 4), 1.0, 0.0)
        given = jnp.concatenate([basis, hot], axis=0).astype(BF16)
        for c in range(0, LAT, CHUNK):
            v = dot(w1t[c : c + CHUNK, :], given)
            t = jnp.tanh(v)
            vt = v * t
            latent[c : c + CHUNK, :] = (v + vt).astype(BF16)
            slope1[k, c : c + CHUNK, :] = ((1.0 + t) * ((1.0 + v) - vt)).astype(BF16)
        made = dot(wct[...], latent[...])
        mix0[k] = made[0:C]
        mix[k] = made[0:C] * env_k
        edge[3, pl.ds(k, 1), :] = made[C : C + 1]
        return carry

    lax.fori_loop(0, K, first, 0)

    def weigh(parts, source_of, out):
        for j in range(0, ATOMS, BA):
            for half in range(0, C, 32):
                total = [None] * 9
                for k in range(K):
                    read = [source_of(k, l, half, j) for l in range(parts)]
                    for m in range(9):
                        term = read[DEGREE[m] if parts == 3 else 0]
                        if m:
                            term = term * harm[m, k : k + 1, j : j + BA]
                        total[m] = term if k == 0 else total[m] + term
                for m in range(9):
                    out[m, half : half + 32, j : j + BA] = total[m] * NORM

    weigh(1, lambda k, l, half, j: mix[k, half : half + 32, j : j + BA], dens)

    def second(k, carry):
        env_k = edge[1, pl.ds(k, 1), :]
        h_rows = [None] + [harm[m, pl.ds(k, 1), :] for m in range(1, 9)]
        for j in range(0, ATOMS, BA):
            h = [None] + [h_rows[m][:, j : j + BA] for m in range(1, 9)]
            mixed = mix[k, :, j : j + BA]
            for l, terms in enumerate(([0], [1, 2, 3], [4, 5, 6, 7, 8])):
                prod = None
                for m in terms:
                    term = dens[m, :, j : j + BA]
                    if m:
                        term = term * h[m]
                    prod = term if prod is None else prod + term
                prods[l * C : l * C + C, j : j + BA] = prod
                scal[l * C : l * C + C, j : j + BA] = (prod * mixed).astype(BF16)
        for c in range(0, LAT, CHUNK):
            v = dot(wut[c : c + CHUNK, :], scal[...])
            t = jnp.tanh(v)
            vt = v * t
            updated[c : c + CHUNK, :] = (v + vt).astype(BF16)
            slope2[c : c + CHUNK, :] = ((1.0 + t) * ((1.0 + v) - vt)).astype(BF16)
        gain = dot(ew16[...], updated[...])
        edge[3, pl.ds(k, 1), :] = edge[3, pl.ds(k, 1), :] + gain[0:1]
        back = dot(wue[...], slope2[...])
        rows = [[] for _ in range(9)]
        for j in range(0, ATOMS, BA):
            env_j = env_k[:, j : j + BA]
            mixed = mix[k, :, j : j + BA]
            partial = None
            flows = []
            for l in range(3):
                flow = back[l * C : l * C + C, j : j + BA] * env_j
                term = flow * prods[l * C : l * C + C, j : j + BA]
                partial = term if partial is None else partial + term
                flow = flow * mixed
                dscal[k, l * C : l * C + C, j : j + BA] = flow
                flows.append(flow)
            dmix[k, :, j : j + BA] = partial
            for m in range(1, 9):
                rows[m].append(
                    jnp.sum(flows[DEGREE[m]] * dens[m, :, j : j + BA], axis=0, keepdims=True)
                )
        for m in range(1, 9):
            dharm[m, pl.ds(k, 1), :] = jnp.concatenate(rows[m], axis=1)
        return carry

    lax.fori_loop(0, K, second, 0)

    weigh(3, lambda k, l, half, j: dscal[k, l * C + half : l * C + half + 32, j : j + BA], ddens)

    def third(k, carry):
        sq_k = edge[0, pl.ds(k, 1), :]
        env_k = edge[1, pl.ds(k, 1), :]
        h_rows = [None] + [harm[m, pl.ds(k, 1), :] for m in range(1, 9)]
        rows = [[] for _ in range(9)]
        for j in range(0, ATOMS, BA):
            mixed = mix[k, :, j : j + BA]
            total = dmix[k, :, j : j + BA] + ddens[0, :, j : j + BA]
            for m in range(1, 9):
                slope = ddens[m, :, j : j + BA]
                total = total + slope * h_rows[m][:, j : j + BA]
                rows[m].append(jnp.sum(mixed * slope, axis=0, keepdims=True))
            rows[0].append(jnp.sum(total * mix0[k, :, j : j + BA], axis=0, keepdims=True))
            dlow[0:C, j : j + BA] = (total * env_k[:, j : j + BA]).astype(BF16)
        edge[4, pl.ds(k, 1), :] = jnp.concatenate(rows[0], axis=1)
        for m in range(1, 9):
            dharm[m, pl.ds(k, 1), :] = dharm[m, pl.ds(k, 1), :] + jnp.concatenate(rows[m], axis=1)
        high = env_k.astype(BF16).astype(F32)
        tail = jnp.where(
            lax.broadcasted_iota(jnp.int32, (16, ATOMS), 0) == 0,
            high,
            jnp.where(lax.broadcasted_iota(jnp.int32, (16, ATOMS), 0) == 1, env_k - high, 0.0),
        )
        dlow[C : C + 16, :] = tail.astype(BF16)
        for c in range(0, LAT, CHUNK):
            d = dot(wcc[c : c + CHUNK, :], dlow[...])
            dpre[c : c + CHUNK, :] = (d * slope1[k, c : c + CHUNK, :].astype(F32)).astype(BF16)
        db = dot(w1[...], dpre[...])[0:8]
        db = db * jnp.exp(-rates * sq_k)
        edge[5, pl.ds(k, 1), :] = jnp.sum(db, axis=0, keepdims=True)
        edge[6, pl.ds(k, 1), :] = jnp.sum(db * rates, axis=0, keepdims=True)
        return carry

    lax.fori_loop(0, K, third, 0)

    sums = edge[3]
    energies[0] = jnp.sum(sums * env, axis=0, keepdims=True)
    denv = sums + edge[4] + edge[5]
    dsq = (-edge[6]) * env + denv * live * cut * (-2.0 / 64.0)
    dh = [None] + [dharm[m] for m in range(1, 9)]
    gx = SCALE * (dh[1] + ROOT3 * (uy * dh[4] + uz * dh[7] + ux * dh[8]) - ux * dh[6]) + 2.0 * rx * dsq
    gy = SCALE * (dh[2] + ROOT3 * (ux * dh[4] + uz * dh[5] - uy * dh[8]) - uy * dh[6]) + 2.0 * ry * dsq
    gz = SCALE * (dh[3] + ROOT3 * (uy * dh[5] + ux * dh[7]) + 2.0 * uz * dh[6]) + 2.0 * rz * dsq
    grads = (gx, gy, gz)
    terms = [r * g for r in (rx, ry, rz) for g in grads] + list(grads)
    for v, term in enumerate(terms):
        for j in range(ATOMS // BA):
            vals[j, 8 * v : 8 * v + 8, :] = term[:, j * BA : j * BA + BA]
    vals[:, 96:128, :] = jnp.zeros((ATOMS // BA, 32, BA), F32)

    ghost[...] = jnp.zeros_like(ghost)

    def scatter(k, carry):
        group = jnp.broadcast_to(nbr[0, 0, pl.ds(k, 1), :] // SPAN, (16, ATOMS))
        term = jnp.concatenate(
            [vals[j, pl.ds(k, 16, stride=8), :] for j in range(ATOMS // BA)], axis=1
        )
        spread = jnp.concatenate(
            [jnp.where(group == g, term, 0.0).astype(BF16) for g in range(GROUPS)], axis=0
        )
        ghost[...] += dot_nt(spread, onehot[k]).reshape(9, 32, SPAN)
        return carry

    lax.fori_loop(0, K, scatter, 0)

    outs = []
    for slot, (dr, dc) in enumerate(NEAR):
        copy = pltpu.make_async_remote_copy(
            src_ref=ghost.at[(dr + 1) * 3 + dc + 1],
            dst_ref=ghost_in.at[slot],
            send_sem=send_out.at[slot],
            recv_sem=recv_out.at[slot],
            device_id=at(dr, dc),
            device_id_type=MESH,
        )
        copy.start()
        outs.append(copy)
    own_sums = jnp.concatenate([jnp.sum(t, axis=0, keepdims=True) for t in terms], axis=0)
    total = ghost[4]
    for slot, copy in enumerate(outs):
        copy.wait_recv()
        total = total + ghost_in[slot]
    total = jnp.concatenate([total[0:12], total[16:28]], axis=1)
    forces[0, 0] = own_sums[9:12] - total[9:12]
    virial[0, 0] = -0.5 * (own_sums[0:9] + total[0:9])
    for copy in sends + outs:
        copy.wait_send()


def solution(mesh):
    n_row, n_col = mesh.shape["row"], mesh.shape["col"]
    vmem = pl.BlockSpec(memory_space=pltpu.VMEM)
    smem = pl.BlockSpec(memory_space=pltpu.SMEM)

    def on_device(pos, spc, valid, rcount, ccount, nbr, rate, rw, ct, nt, cw, uw, ew):
        return pl.pallas_call(
            functools.partial(kernel, n_row, n_col),
            out_shape=(
                jax.ShapeDtypeStruct((1, 1, 3, ATOMS), F32),
                jax.ShapeDtypeStruct((1, 1, 9, ATOMS), F32),
                jax.ShapeDtypeStruct((1, 1, ATOMS), F32),
            ),
            in_specs=[vmem] * 6 + [smem] + [vmem] * 6,
            out_specs=(vmem, vmem, vmem),
            scratch_shapes=[
                pltpu.VMEM((8, 2 * BA), F32),
                pltpu.VMEM((len(REACH), 8, 2 * BA), F32),
                pltpu.VMEM((2, 8 * GROUPS, SPAN), F32),
                pltpu.VMEM((ATOMS // BA, 8 * K, BA), F32),
                pltpu.VMEM((K, SPAN, ATOMS), BF16),
                pltpu.VMEM((9, K, ATOMS), F32),
                pltpu.VMEM((8, K, ATOMS), F32),
                pltpu.VMEM((128, LAT), F32),
                pltpu.VMEM((LAT, 16), BF16),
                pltpu.VMEM((16, LAT), BF16),
                pltpu.VMEM((LAT, 3 * C), BF16),
                pltpu.VMEM((3 * C, LAT), BF16),
                pltpu.VMEM((80, LAT), BF16),
                pltpu.VMEM((LAT, 80), BF16),
                pltpu.VMEM((16, LAT), BF16),
                pltpu.VMEM((LAT, ATOMS), BF16),
                pltpu.VMEM((K, LAT, ATOMS), BF16),
                pltpu.VMEM((LAT, ATOMS), BF16),
                pltpu.VMEM((LAT, ATOMS), BF16),
                pltpu.VMEM((K, C, ATOMS), F32),
                pltpu.VMEM((K, C, ATOMS), F32),
                pltpu.VMEM((9, C, ATOMS), F32),
                pltpu.VMEM((9, C, ATOMS), F32),
                pltpu.VMEM((3 * C, ATOMS), F32),
                pltpu.VMEM((3 * C, ATOMS), BF16),
                pltpu.VMEM((K, 3 * C, ATOMS), F32),
                pltpu.VMEM((K, C, ATOMS), F32),
                pltpu.VMEM((9, K, ATOMS), F32),
                pltpu.VMEM((80, ATOMS), BF16),
                pltpu.VMEM((LAT, ATOMS), BF16),
                pltpu.VMEM((ATOMS // BA, 128, BA), F32),
                pltpu.VMEM((9, 32, SPAN), F32),
                pltpu.VMEM((8, 32, SPAN), F32),
                pltpu.SemaphoreType.DMA((len(REACH),)),
                pltpu.SemaphoreType.DMA((len(REACH),)),
                pltpu.SemaphoreType.DMA((len(NEAR),)),
                pltpu.SemaphoreType.DMA((len(NEAR),)),
            ],
            compiler_params=pltpu.CompilerParams(
                collective_id=0, has_side_effects=True, vmem_limit_bytes=48 * 1024 * 1024
            ),
        )(pos, spc, valid, rcount, ccount, nbr, rate, rw, ct, nt, cw, uw, ew.reshape(1, LAT))

    in_specs = (
        P("row", "col", None, None),
        P("row", "col", None),
        P("row", "col", None),
        P("row", "col"),
        P("row", "col"),
        P("row", "col", None, None),
    ) + (P(),) * 7
    out_specs = (P("row", "col", None, None), P("row", "col", None, None), P("row", "col", None))
    return jax.shard_map(on_device, mesh=mesh, in_specs=in_specs, out_specs=out_specs, check_vma=False)
```

```python
import functools
import math

import jax
import jax.numpy as jnp
from jax import lax
from jax.experimental import pallas as pl
from jax.experimental.pallas import tpu as pltpu
from jax.sharding import PartitionSpec as P

K = 8
BA = 128
C = 64
LAT = 512
ATOMS = 512
SPAN = 256
GROUPS = 18
SLAB = 8.0
SCALE = 0.25
ROOT3 = math.sqrt(3.0)
NORM = 1.0 / math.sqrt(8.0)
F32 = jnp.float32
BF16 = jnp.bfloat16
MESH = pl.DeviceIdType.MESH

NEAR = [(a, b) for a in (-1, 0, 1) for b in (-1, 0, 1) if (a, b) != (0, 0)]
REACH = NEAR + [(2, b) for b in (-1, 0, 1)] + [(a, 2) for a in (-1, 0, 1)]
DEGREE = [0, 1, 1, 1, 2, 2, 2, 2, 2]
HALF = 256


def dot(a, b):
    return lax.dot_general(a, b, (((1,), (0,)), ((), ())), preferred_element_type=F32)


def dot_nt(a, b):
    return lax.dot_general(a, b, (((1,), (1,)), ((), ())), preferred_element_type=F32)


def kernel(
    n_row,
    n_col,
    pos,
    spc,
    valid,
    rcount,
    ccount,
    nbr,
    rate,
    rw,
    ct,
    nt,
    cw,
    uw,
    ew,
    result,
    pos_v,
    spc_v,
    valid_v,
    rcount_v,
    ccount_v,
    nbr_v,
    rate_v,
    rw_v,
    ct_v,
    nt_v,
    cw_v,
    uw_v,
    ew_v,
    load_sem,
    own,
    inbox,
    near_stage,
    near_table,
    rel_code,
    onehot,
    harm,
    edge,
    w_stage,
    w1t,
    w1,
    wut,
    wue,
    wct,
    wcc,
    ew_wide,
    given,
    latent,
    slope1,
    slope2,
    mix0,
    mix,
    dens,
    ddens,
    prods,
    scal,
    dscal,
    dmix,
    dharm,
    dlow,
    dpre,
    vals,
    ghost,
    ghost_in,
    send_in,
    recv_in,
    send_out,
    recv_out,
):
    row = lax.axis_index("row")
    col = lax.axis_index("col")

    def at(dr, dc):
        return (lax.rem(row + (dr + n_row), n_row), lax.rem(col + (dc + n_col), n_col))

    barrier = pltpu.get_barrier_semaphore()
    for dr, dc in REACH:
        pl.semaphore_signal(barrier, inc=1, device_id=at(-dr, -dc), device_id_type=MESH)

    loads = [
        pltpu.make_async_copy(there, here, load_sem.at[i])
        for i, (there, here) in enumerate(
            [
                (pos, pos_v),
                (spc, spc_v),
                (valid, valid_v),
                (rcount, rcount_v),
                (ccount, ccount_v),
                (nbr, nbr_v),
                (rate, rate_v),
                (rw, rw_v),
                (ct, ct_v),
                (nt, nt_v),
                (cw, cw_v),
                (uw, uw_v),
                (ew, ew_v),
            ]
        )
    ]
    for load in loads:
        load.start()
    for load in loads[:5]:
        load.wait()

    code = (valid_v[0] * (spc_v[0] + 1)).astype(F32)
    moves = jnp.concatenate(
        [
            jnp.where(jnp.broadcast_to(ccount_v[...], (1, BA)) > 0, 1.0, 0.0),
            jnp.where(jnp.broadcast_to(rcount_v[...], (1, BA)) > 0, 1.0, 0.0),
        ],
        axis=1,
    )
    for i in range(3):
        own[i : i + 1, :] = pos_v[0, i]
        own[i + 4 : i + 5, :] = pos_v[0, i]
    own[3:4, :] = code * moves
    own[7:8, :] = code * (1.0 - moves)
    pl.semaphore_wait(barrier, len(REACH))
    sends = []
    for slot, (dr, dc) in enumerate(REACH):
        copy = pltpu.make_async_remote_copy(
            src_ref=own,
            dst_ref=inbox.at[slot],
            send_sem=send_in.at[slot],
            recv_sem=recv_in.at[slot],
            device_id=at(dr, dc),
            device_id_type=MESH,
        )
        copy.start()
        sends.append(copy)

    for load in loads[5:]:
        load.wait()
    w_stage[...] = jnp.zeros_like(w_stage)
    w_stage[0:8, :] = rw_v[...].astype(F32) * 0.5
    w_stage[8:10, :] = ct_v[...].astype(F32) * 0.5
    w_stage[10:12, :] = nt_v[...].astype(F32) * 0.5
    w1[...] = w_stage[0:16, :].astype(BF16)
    w1t[...] = w_stage[...].T[:, 0:16].astype(BF16)
    half_u = uw_v[...].astype(F32) * 0.5
    ew_row = ew_v[...].astype(F32).reshape(1, LAT)
    wue[...] = (half_u * ew_row).astype(BF16)
    wut[...] = half_u.T.astype(BF16)
    w_stage[0:C, :] = cw_v[...].astype(F32)
    w_stage[C : C + 1, :] = ew_row
    w_stage[C + 1 : C + 2, :] = ew_row
    wct[...] = w_stage[0:80, :].astype(BF16)
    turned = w_stage[...].T
    wcc[...] = turned[:, 0:80].astype(BF16)
    ew_wide[...] = jnp.broadcast_to(turned[:, C : C + 1], (LAT, BA))

    place_of = lax.broadcasted_iota(jnp.int32, (SPAN, ATOMS), 0)

    for k in range(K):
        place = nbr_v[0, 0, k : k + 1, :] & (SPAN - 1)
        onehot[k] = jnp.where(place_of == place, 1.0, 0.0).astype(BF16)

    for copy in sends:
        copy.wait_recv()

    row_of = lax.broadcasted_iota(jnp.int32, (8, BA), 0)

    def source(dr, dc):
        if (dr, dc) == (0, 0):
            return own
        return inbox.at[REACH.index((-dr, -dc))]

    centre = None
    for p in range(9):
        a, b = p // 3 - 1, p % 3 - 1
        tiles = []
        for half, brought, dx, dy in (
            (0, source(a - 1, b)[:, BA:], -SLAB, 0.0),
            (1, source(a, b - 1)[:, :BA], 0.0, -SLAB),
        ):
            tile = jnp.where(row_of < 4, brought, source(a, b)[:, half * BA : half * BA + BA])
            shift = jnp.where(row_of == 4, SLAB * a, jnp.where(row_of == 5, SLAB * b, 0.0))
            shift = jnp.where(row_of == 0, SLAB * a + dx, jnp.where(row_of == 1, SLAB * b + dy, shift))
            tiles.append(tile + shift)
        tile = jnp.concatenate(tiles, axis=1)
        high = tile.astype(BF16).astype(F32)
        near_stage[8 * p : 8 * p + 8, :] = high
        near_stage[72 + 8 * p : 80 + 8 * p, :] = tile - high
        if p == 4:
            centre = jnp.concatenate([tile, pltpu.roll(tile, 4, 0)], axis=1)
    near_table[...] = near_stage[...].astype(BF16)
    row8 = lax.broadcasted_iota(jnp.int32, (8, ATOMS), 0)
    centre_xyz = jnp.where(row8 < 3, centre, 0.0)
    centre_code = centre[3:4, :]

    for k in range(K):
        index = jnp.broadcast_to(nbr_v[0, 0, k : k + 1, :], (8, ATOMS))
        block = lax.shift_right_logical(index, 9)
        found = dot(near_table[...], onehot[k])
        picked = found[0:8] + found[72:80]
        for p in range(1, 9):
            picked = jnp.where(block == p, found[8 * p : 8 * p + 8] + found[72 + 8 * p : 80 + 8 * p], picked)
        picked = jnp.where((index & SPAN) != 0, pltpu.roll(picked, 4, 0), picked) - centre_xyz
        for j in range(ATOMS // BA):
            rel_code[j, 8 * k : 8 * k + 8, :] = picked[:, j * BA : j * BA + BA]

    rx, ry, rz, ncode = [
        jnp.concatenate([rel_code[j, pl.ds(c, K, stride=8), :] for j in range(ATOMS // BA)], axis=1)
        for c in range(4)
    ]
    live = jnp.where(jnp.logical_and(ncode > 0.5, centre_code > 0.5), 1.0, 0.0)
    sq = rx * rx + ry * ry + rz * rz
    cut = jnp.maximum(1.0 - sq * (1.0 / 64.0), 0.0)
    env = cut * cut * live
    ux, uy, uz = rx * SCALE, ry * SCALE, rz * SCALE
    norm = ux * ux + uy * uy + uz * uz
    for m, h in enumerate(
        [
            ux,
            uy,
            uz,
            ROOT3 * ux * uy,
            ROOT3 * uy * uz,
            0.5 * (3.0 * uz * uz - norm),
            ROOT3 * ux * uz,
            0.5 * ROOT3 * (ux * ux - uy * uy),
        ]
    ):
        harm[m + 1] = h
    edge[0] = sq
    edge[1] = env
    edge[2] = ncode

    rates = jnp.zeros((8, ATOMS), F32)
    for n in range(8):
        rates = jnp.where(row8 == n, rate_v[n], rates)
    kind = jnp.where(row8 % 2 == 0, 1.0, 2.0)

    def first_chain(k, h):
        v = dot(w1t[...], given[k, :, h : h + HALF])
        t = jnp.tanh(v)
        vt = v * t
        latent[k, :, h : h + HALF] = (v + vt).astype(BF16)
        slope1[k, :, h : h + HALF] = ((1.0 + t) * ((1.0 + v) - vt)).astype(BF16)

    def first_mix(k, h):
        made = dot(wct[...], latent[k, :, h : h + HALF])
        mix0[k, :, h : h + HALF] = made[0:C]
        mix[k, :, h : h + HALF] = made[0:C] * edge[1, k : k + 1, h : h + HALF]
        edge[3, k : k + 1, h : h + HALF] = made[C : C + 1]

    for k in range(K):
        basis = jnp.exp(-rates * sq[k : k + 1, :]) * env[k : k + 1, :]
        codes = jnp.where(row8 < 2, centre_code, ncode[k : k + 1, :])
        hot = jnp.where(jnp.logical_and(codes == kind, row8 < 4), 1.0, 0.0)
        given[k] = jnp.concatenate([basis, hot], axis=0).astype(BF16)
    for step in range(K + 1):
        for h in (0, HALF):
            if step < K:
                first_chain(step, h)
            if step > 0:
                first_mix(step - 1, h)

    def weigh(parts, source_of, out):
        for j in range(0, ATOMS, BA):
            for half in range(0, C, 32):
                total = [None] * 9
                for k in range(K):
                    read = [source_of(k, l, half, j) for l in range(parts)]
                    for m in range(9):
                        term = read[DEGREE[m] if parts == 3 else 0]
                        if m:
                            term = term * harm[m, k : k + 1, j : j + BA]
                        total[m] = term if k == 0 else total[m] + term
                for m in range(9):
                    out[m, half : half + 32, j : j + BA] = total[m] * NORM

    weigh(1, lambda k, l, half, j: mix[k, half : half + 32, j : j + BA], dens)

    def second_in(k, j):
        h = [None] + [harm[m, k : k + 1, j : j + BA] for m in range(1, 9)]
        mixed = mix[k, :, j : j + BA]
        for l, terms in enumerate(([0], [1, 2, 3], [4, 5, 6, 7, 8])):
            prod = None
            for m in terms:
                term = dens[m, :, j : j + BA]
                if m:
                    term = term * h[m]
                prod = term if prod is None else prod + term
            prods[k, l * C : l * C + C, j : j + BA] = prod
            scal[k, l * C : l * C + C, j : j + BA] = (prod * mixed).astype(BF16)

    def second_chain(k, h):
        v = dot(wut[...], scal[k, :, h : h + HALF])
        t = jnp.tanh(v)
        vt = v * t
        updated = v + vt
        slope2[k, :, h : h + HALF] = ((1.0 + t) * ((1.0 + v) - vt)).astype(BF16)
        for j in range(0, HALF, BA):
            gain = jnp.sum(updated[:, j : j + BA] * ew_wide[...], axis=0, keepdims=True)
            edge[7, k : k + 1, h + j : h + j + BA] = gain

    def second_out(k, h):
        back = dot(wue[...], slope2[k, :, h : h + HALF])
        for j in range(0, HALF, BA):
            at_j = slice(h + j, h + j + BA)
            env_j = edge[1, k : k + 1, at_j]
            both = mix[k, :, at_j] * env_j
            partial = None
            for l in range(3):
                flow = back[l * C : l * C + C, j : j + BA]
                term = flow * prods[k, l * C : l * C + C, at_j]
                partial = term if partial is None else partial + term
                dscal[k, l * C : l * C + C, at_j] = flow * both
            dmix[k, :, at_j] = partial * env_j

    for step in range(-1, K + 1):
        for h in (0, HALF):
            if 0 <= step < K:
                second_chain(step, h)
            if step + 1 < K:
                second_in(step + 1, h)
                second_in(step + 1, h + BA)
            if step > 0:
                second_out(step - 1, h)

    weigh(3, lambda k, l, half, j: dscal[k, l * C + half : l * C + half + 32, j : j + BA], ddens)

    def fold(x):
        return jnp.sum(x.reshape(8, 8, BA), axis=0)

    def rows_of(parts):
        pairs = [
            jnp.where(row_of < 4, parts[i], parts[i + 4])
            + pltpu.roll(jnp.where(row_of < 4, parts[i + 4], parts[i]), 4, 0)
            for i in range(4)
        ]
        for size in (2, 1):
            pairs = [
                jnp.where(
                    row_of % (2 * size) < size,
                    pairs[i] + pltpu.roll(pairs[i], 8 - size, 0),
                    pairs[i + size] + pltpu.roll(pairs[i + size], size, 0),
                )
                for i in range(size)
            ]
        return pairs[0]

    def third_in(k, j):
        at_j = slice(j, j + BA)
        mixed = mix[k, :, at_j]
        flows = [dscal[k, l * C : l * C + C, at_j] for l in range(3)]
        total = dmix[k, :, at_j] + ddens[0, :, at_j]
        parts = []
        for m in range(1, 9):
            slope = ddens[m, :, at_j]
            total = total + slope * harm[m, k : k + 1, at_j]
            parts.append(fold(mixed * slope + flows[DEGREE[m]] * dens[m, :, at_j]))
        dharm[j // BA, 8 * k : 8 * k + 8, :] = rows_of(parts)
        edge[4, k : k + 1, at_j] = jnp.sum(total * mix0[k, :, at_j], axis=0, keepdims=True)
        dlow[k, 0:C, at_j] = (total * edge[1, k : k + 1, at_j]).astype(BF16)

    def third_chain(k, h):
        d = dot(wcc[...], dlow[k, :, h : h + HALF])
        dpre[k, :, h : h + HALF] = (d * slope1[k, :, h : h + HALF].astype(F32)).astype(BF16)

    def third_out(k, h):
        db = dot(w1[...], dpre[k, :, h : h + HALF])[0:8]
        db = db * jnp.exp(-rates[:, h : h + HALF] * edge[0, k : k + 1, h : h + HALF])
        edge[5, k : k + 1, h : h + HALF] = jnp.sum(db, axis=0, keepdims=True)
        edge[6, k : k + 1, h : h + HALF] = jnp.sum(db * rates[:, h : h + HALF], axis=0, keepdims=True)

    row16 = lax.broadcasted_iota(jnp.int32, (16, ATOMS), 0)
    for k in range(K):
        env_k = env[k : k + 1, :]
        high = env_k.astype(BF16).astype(F32)
        tail = jnp.where(row16 == 0, high, jnp.where(row16 == 1, env_k - high, 0.0))
        dlow[k, C : C + 16, :] = tail.astype(BF16)
    for step in range(-1, K + 1):
        for h in (0, HALF):
            if 0 <= step < K:
                third_chain(step, h)
            if step + 1 < K:
                third_in(step + 1, h)
                third_in(step + 1, h + BA)
            if step > 0:
                third_out(step - 1, h)

    sums = edge[3] + edge[7]
    result[12, :, :] = jnp.sum(sums * env, axis=0, keepdims=True)
    denv = sums + edge[4] + edge[5]
    dsq = (-edge[6]) * env + denv * live * cut * (-2.0 / 64.0)
    dh = [None] + [
        jnp.concatenate([dharm[j, pl.ds(m, K, stride=8), :] for j in range(ATOMS // BA)], axis=1)
        for m in range(8)
    ]
    gx = SCALE * (dh[1] + ROOT3 * (uy * dh[4] + uz * dh[7] + ux * dh[8]) - ux * dh[6]) + 2.0 * rx * dsq
    gy = SCALE * (dh[2] + ROOT3 * (ux * dh[4] + uz * dh[5] - uy * dh[8]) - uy * dh[6]) + 2.0 * ry * dsq
    gz = SCALE * (dh[3] + ROOT3 * (uy * dh[5] + ux * dh[7]) + 2.0 * uz * dh[6]) + 2.0 * rz * dsq
    grads = (gx, gy, gz)
    terms = [r * g for r in (rx, ry, rz) for g in grads] + list(grads)
    for v, term in enumerate(terms):
        for j in range(ATOMS // BA):
            vals[j, 8 * v : 8 * v + 8, :] = term[:, j * BA : j * BA + BA]
    vals[:, 96:128, :] = jnp.zeros((ATOMS // BA, 32, BA), F32)

    for k in range(K):
        group = jnp.broadcast_to(lax.shift_right_logical(nbr_v[0, 0, k : k + 1, :], 8), (8, ATOMS))
        term = jnp.concatenate(
            [vals[j, pl.ds(k, 16, stride=8), :] for j in range(ATOMS // BA)], axis=1
        )
        upper = term[0:8]
        lower = term[8:16] + pltpu.roll(term[8:16], 4, 0)
        later = group - jnp.where(row8 < 4, 0, 1)
        pieces = [jnp.where(group == g, upper, 0.0) for g in range(GROUPS)]
        pieces += [jnp.where(later == g, lower, 0.0) for g in range(0, GROUPS, 2)]
        spread = jnp.concatenate(pieces, axis=0).astype(BF16)
        found = dot_nt(spread, onehot[k])
        first_part = found[0:144].reshape(9, 16, SPAN)
        second_part = found[144:216].reshape(9, 8, SPAN)
        if k == 0:
            ghost[:, 0:16, :] = first_part
            ghost[:, 16:24, :] = second_part
        else:
            ghost[:, 0:16, :] += first_part
            ghost[:, 16:24, :] += second_part

    outs = []
    for slot, (dr, dc) in enumerate(NEAR):
        copy = pltpu.make_async_remote_copy(
            src_ref=ghost.at[(dr + 1) * 3 + dc + 1],
            dst_ref=ghost_in.at[slot],
            send_sem=send_out.at[slot],
            recv_sem=recv_out.at[slot],
            device_id=at(dr, dc),
            device_id_type=MESH,
        )
        copy.start()
        outs.append(copy)
    own_sums = jnp.concatenate([jnp.sum(t, axis=0, keepdims=True) for t in terms], axis=0)
    total = ghost[4]
    for slot, copy in enumerate(outs):
        copy.wait_recv()
        total = total + ghost_in[slot]
    total = jnp.concatenate(
        [
            jnp.concatenate([total[0:8], total[16:20]], axis=0),
            jnp.concatenate([total[8:16], total[20:24]], axis=0),
        ],
        axis=1,
    )
    total = jnp.where(
        lax.broadcasted_iota(jnp.int32, (12, ATOMS), 0) < 9,
        -0.5 * (own_sums + total),
        own_sums - total,
    )
    for v in range(12):
        result[v, :, :] = total[v : v + 1]
    for copy in sends + outs:
        copy.wait_send()


def share_out(result, forces, virial, energies):
    virial[...] = result[0:9]
    forces[...] = result[9:12]
    energies[...] = result[12:13]


def solution(mesh):
    n_row, n_col = mesh.shape["row"], mesh.shape["col"]
    hbm = pl.BlockSpec(memory_space=pltpu.HBM)

    def on_device(pos, spc, valid, rcount, ccount, nbr, rate, rw, ct, nt, cw, uw, ew):
        args = (pos.transpose(0, 2, 1, 3), spc, valid, rcount, ccount, nbr, rate, rw, ct, nt, cw.T, uw, ew)
        held = [pltpu.VMEM(a.shape, a.dtype) for a in args]
        held[6] = pltpu.SMEM(rate.shape, rate.dtype)
        result = pl.pallas_call(
            functools.partial(kernel, n_row, n_col),
            out_shape=jax.ShapeDtypeStruct((13, 1, ATOMS), F32),
            in_specs=[hbm] * len(args),
            out_specs=pl.BlockSpec(memory_space=pltpu.VMEM),
            scratch_shapes=held
            + [
                pltpu.SemaphoreType.DMA((13,)),
                pltpu.VMEM((8, 2 * BA), F32),
                pltpu.VMEM((len(REACH), 8, 2 * BA), F32),
                pltpu.VMEM((144, SPAN), F32),
                pltpu.VMEM((144, SPAN), BF16),
                pltpu.VMEM((ATOMS // BA, 8 * K, BA), F32),
                pltpu.VMEM((K, SPAN, ATOMS), BF16),
                pltpu.VMEM((9, K, ATOMS), F32),
                pltpu.VMEM((8, K, ATOMS), F32),
                pltpu.VMEM((128, LAT), F32),
                pltpu.VMEM((LAT, 16), BF16),
                pltpu.VMEM((16, LAT), BF16),
                pltpu.VMEM((LAT, 3 * C), BF16),
                pltpu.VMEM((3 * C, LAT), BF16),
                pltpu.VMEM((80, LAT), BF16),
                pltpu.VMEM((LAT, 80), BF16),
                pltpu.VMEM((LAT, BA), F32),
                pltpu.VMEM((K, 16, ATOMS), BF16),
                pltpu.VMEM((K, LAT, ATOMS), BF16),
                pltpu.VMEM((K, LAT, ATOMS), BF16),
                pltpu.VMEM((K, LAT, ATOMS), BF16),
                pltpu.VMEM((K, C, ATOMS), F32),
                pltpu.VMEM((K, C, ATOMS), F32),
                pltpu.VMEM((9, C, ATOMS), F32),
                pltpu.VMEM((9, C, ATOMS), F32),
                pltpu.VMEM((K, 3 * C, ATOMS), F32),
                pltpu.VMEM((K, 3 * C, ATOMS), BF16),
                pltpu.VMEM((K, 3 * C, ATOMS), F32),
                pltpu.VMEM((K, C, ATOMS), F32),
                pltpu.VMEM((ATOMS // BA, 8 * K, BA), F32),
                pltpu.VMEM((K, 80, ATOMS), BF16),
                pltpu.VMEM((K, LAT, ATOMS), BF16),
                pltpu.VMEM((ATOMS // BA, 128, BA), F32),
                pltpu.VMEM((9, 24, SPAN), F32),
                pltpu.VMEM((8, 24, SPAN), F32),
                pltpu.SemaphoreType.DMA((len(REACH),)),
                pltpu.SemaphoreType.DMA((len(REACH),)),
                pltpu.SemaphoreType.DMA((len(NEAR),)),
                pltpu.SemaphoreType.DMA((len(NEAR),)),
            ],
            compiler_params=pltpu.CompilerParams(
                collective_id=0, has_side_effects=True, vmem_limit_bytes=64 * 1024 * 1024
            ),
        )(*args)
        forces, virial, energies = pl.pallas_call(
            share_out,
            out_shape=[jax.ShapeDtypeStruct((n, 1, ATOMS), F32) for n in (3, 9, 1)],
            in_specs=[pl.BlockSpec(memory_space=pltpu.VMEM)],
            out_specs=[pl.BlockSpec(memory_space=pltpu.VMEM)] * 3,
            compiler_params=pltpu.CompilerParams(vmem_limit_bytes=1 << 20),
        )(result)
        return (
            forces.reshape(1, 3, 1, ATOMS).transpose(0, 2, 1, 3),
            virial.reshape(1, 9, 1, ATOMS).transpose(0, 2, 1, 3),
            energies,
        )

    in_specs = (
        P("row", "col", None, None),
        P("row", "col", None),
        P("row", "col", None),
        P("row", "col"),
        P("row", "col"),
        P("row", "col", None, None),
    ) + (P(),) * 7
    out_specs = (P("row", "col", None, None), P("row", "col", None, None), P("row", "col", None))
    return jax.shard_map(on_device, mesh=mesh, in_specs=in_specs, out_specs=out_specs, check_vma=False)
```

```python
import functools
import math

import jax
import jax.numpy as jnp
from jax import lax
from jax.experimental import pallas as pl
from jax.experimental.pallas import tpu as pltpu
from jax.sharding import PartitionSpec as P

K = 8
BA = 128
C = 64
LAT = 512
ATOMS = 512
SPAN = 256
GROUPS = 18
SLAB = 8.0
SCALE = 0.25
ROOT3 = math.sqrt(3.0)
NORM = 1.0 / math.sqrt(8.0)
F32 = jnp.float32
BF16 = jnp.bfloat16
MESH = pl.DeviceIdType.MESH

NEAR = [(a, b) for a in (-1, 0, 1) for b in (-1, 0, 1) if (a, b) != (0, 0)]
REACH = NEAR + [(2, b) for b in (-1, 0, 1)] + [(a, 2) for a in (-1, 0, 1)]
DEGREE = [0, 1, 1, 1, 2, 2, 2, 2, 2]
HALF = 256
STRIP = 16
ROWS = 64
BITE = 32


def dot(a, b):
    return lax.dot_general(a, b, (((1,), (0,)), ((), ())), preferred_element_type=F32)


def kernel(
    n_row,
    n_col,
    pos,
    spc,
    valid,
    rcount,
    ccount,
    nbr,
    rate,
    rw,
    ct,
    nt,
    cw,
    uw,
    ew,
    result,
    pos_v,
    spc_v,
    valid_v,
    rcount_v,
    ccount_v,
    nbr_v,
    rate_v,
    rw_v,
    ct_v,
    nt_v,
    cw_v,
    uw_v,
    ew_v,
    load_sem,
    own,
    inbox,
    near_stage,
    near_table,
    rel_code,
    onehot,
    turned_hot,
    harm,
    edge,
    wide_env,
    w_stage,
    w1t,
    w1,
    wut,
    wue,
    wct,
    wcc,
    ew_wide,
    given,
    latent,
    slope1,
    slope2,
    mix0,
    mix,
    dens,
    ddens,
    prods,
    scal,
    dscal,
    dmix,
    dharm,
    folded,
    gain1,
    gain2,
    gain3,
    dbasis,
    dlow,
    dpre,
    vals,
    ghost,
    ghost_in,
    send_in,
    recv_in,
    send_out,
    recv_out,
):
    row = lax.axis_index("row")
    col = lax.axis_index("col")

    def at(dr, dc):
        return (lax.rem(row + (dr + n_row), n_row), lax.rem(col + (dc + n_col), n_col))

    loads = [
        pltpu.make_async_copy(there, here, load_sem.at[i])
        for i, (there, here) in enumerate(
            [
                (pos, pos_v),
                (spc, spc_v),
                (valid, valid_v),
                (rcount, rcount_v),
                (ccount, ccount_v),
                (nbr, nbr_v),
                (rate, rate_v),
                (rw, rw_v),
                (ct, ct_v),
                (nt, nt_v),
                (cw, cw_v),
                (uw, uw_v),
                (ew, ew_v),
            ]
        )
    ]
    for load in loads[:5]:
        load.start()
    barrier = pltpu.get_barrier_semaphore()
    for dr, dc in REACH:
        pl.semaphore_signal(barrier, inc=1, device_id=at(-dr, -dc), device_id_type=MESH)
    for load in loads[5:]:
        load.start()
    for load in loads[:5]:
        load.wait()

    code = (valid_v[0] * (spc_v[0] + 1)).astype(F32)
    moves = jnp.concatenate(
        [
            jnp.where(jnp.broadcast_to(ccount_v[...], (1, BA)) > 0, 1.0, 0.0),
            jnp.where(jnp.broadcast_to(rcount_v[...], (1, BA)) > 0, 1.0, 0.0),
        ],
        axis=1,
    )
    code = code * (1.0 - 2.0 * moves)
    for half in range(2):
        at_half = slice(half * BA, half * BA + BA)
        for i in range(3):
            own[4 * half + i : 4 * half + i + 1, :] = pos_v[0, i][:, at_half]
        own[4 * half + 3 : 4 * half + 4, :] = code[:, at_half]
    pl.semaphore_wait(barrier, len(REACH))
    sends = []
    for slot, (dr, dc) in enumerate(REACH):
        copy = pltpu.make_async_remote_copy(
            src_ref=own,
            dst_ref=inbox.at[slot],
            send_sem=send_in.at[slot],
            recv_sem=recv_in.at[slot],
            device_id=at(dr, dc),
            device_id_type=MESH,
        )
        copy.start()
        sends.append(copy)

    for load in loads[5:]:
        load.wait()
    w_stage[...] = jnp.zeros_like(w_stage)
    w_stage[0:8, :] = rw_v[...].astype(F32) * 0.5
    w_stage[8:10, :] = ct_v[...].astype(F32) * 0.5
    w_stage[10:12, :] = nt_v[...].astype(F32) * 0.5
    w1[...] = w_stage[0:16, :].astype(BF16)
    w1t[...] = w_stage[...].T[:, 0:16].astype(BF16)
    half_u = uw_v[...].astype(F32) * 0.5
    ew_row = ew_v[...].astype(F32).reshape(1, LAT)
    wue[...] = (half_u * ew_row).astype(BF16)
    wut[...] = half_u.T.astype(BF16)
    w_stage[0:C, :] = cw_v[...].astype(F32)
    w_stage[C : C + 1, :] = ew_row
    w_stage[C + 1 : C + 2, :] = ew_row
    wct[...] = w_stage[0:80, :].astype(BF16)
    turned = w_stage[...].T
    wcc[...] = turned[:, 0:80].astype(BF16)
    ew_wide[...] = jnp.broadcast_to(turned[:, C : C + 1], (LAT, BA))

    place_of = lax.broadcasted_iota(jnp.int32, (SPAN, ATOMS), 0)

    for k in range(K):
        place = nbr_v[0, 0, k : k + 1, :] & (SPAN - 1)
        marks = jnp.where(place_of == place, 1.0, 0.0)
        onehot[k] = marks.astype(BF16)
        turned_hot[k] = marks.T.astype(BF16)

    for copy in sends:
        copy.wait_recv()

    row_of = lax.broadcasted_iota(jnp.int32, (8, BA), 0)

    def source(dr, dc):
        if (dr, dc) == (0, 0):
            return own
        return inbox.at[REACH.index((-dr, -dc))]

    centre = None
    for p in range(9):
        a, b = p // 3 - 1, p % 3 - 1
        here = source(a, b)[...]
        tiles = []
        for tile, dx, dy in (
            (pltpu.roll(jnp.where(row_of < 4, here, source(a - 1, b)[...]), 4, 0), -SLAB, 0.0),
            (jnp.where(row_of < 4, source(a, b - 1)[...], here), 0.0, -SLAB),
        ):
            tile = jnp.where(row_of == 3, jnp.maximum(-tile, 0.0), tile)
            tile = jnp.where(row_of == 7, jnp.maximum(tile, 0.0), tile)
            shift = jnp.where(row_of == 4, SLAB * a, jnp.where(row_of == 5, SLAB * b, 0.0))
            shift = jnp.where(row_of == 0, SLAB * a + dx, jnp.where(row_of == 1, SLAB * b + dy, shift))
            tiles.append(tile + shift)
        tile = jnp.concatenate(tiles, axis=1)
        high = tile.astype(BF16).astype(F32)
        near_stage[8 * p : 8 * p + 8, :] = high
        near_stage[72 + 8 * p : 80 + 8 * p, :] = tile - high
        if p == 4:
            centre = jnp.concatenate([tile, pltpu.roll(tile, 4, 0)], axis=1)
    near_table[...] = near_stage[...].astype(BF16)
    row8 = lax.broadcasted_iota(jnp.int32, (8, ATOMS), 0)
    centre_xyz = jnp.where(row8 < 3, centre, 0.0)
    centre_code = centre[3:4, :]

    for k in range(K):
        index = jnp.broadcast_to(nbr_v[0, 0, k : k + 1, :], (8, ATOMS))
        block = lax.shift_right_logical(index, 9)
        found = dot(near_table[...], onehot[k])
        picked = found[0:8] + found[72:80]
        for p in range(1, 9):
            picked = jnp.where(block == p, found[8 * p : 8 * p + 8] + found[72 + 8 * p : 80 + 8 * p], picked)
        picked = jnp.where((index & SPAN) != 0, pltpu.roll(picked, 4, 0), picked) - centre_xyz
        for j in range(ATOMS // BA):
            rel_code[j, 8 * k : 8 * k + 8, :] = picked[:, j * BA : j * BA + BA]

    rx, ry, rz, ncode = [
        jnp.concatenate([rel_code[j, pl.ds(c, K, stride=8), :] for j in range(ATOMS // BA)], axis=1)
        for c in range(4)
    ]
    live = jnp.where(jnp.logical_and(ncode > 0.5, centre_code > 0.5), 1.0, 0.0)
    sq = rx * rx + ry * ry + rz * rz
    cut = jnp.maximum(1.0 - sq * (1.0 / 64.0), 0.0)
    env = cut * cut * live
    ux, uy, uz = rx * SCALE, ry * SCALE, rz * SCALE
    norm = ux * ux + uy * uy + uz * uz
    for m, h in enumerate(
        [
            ux,
            uy,
            uz,
            ROOT3 * ux * uy,
            ROOT3 * uy * uz,
            0.5 * (3.0 * uz * uz - norm),
            ROOT3 * ux * uz,
            0.5 * ROOT3 * (ux * ux - uy * uy),
        ]
    ):
        for k in range(K):
            harm[m, k] = jnp.broadcast_to(h[k : k + 1, :], (8, ATOMS))
    for k in range(K):
        wide_env[k] = jnp.broadcast_to(env[k : k + 1, :], (8, ATOMS))
    edge[0] = sq
    edge[1] = env
    edge[2] = ncode

    rates = jnp.zeros((8, ATOMS), F32)
    for n in range(8):
        rates = jnp.where(row8 == n, rate_v[n], rates)
    kind = jnp.where(row8 % 2 == 0, 1.0, 2.0)

    def fold(x):
        return jnp.sum(x.reshape(x.shape[0] // 8, 8, BA), axis=0)

    def by_row(x, rows):
        return (x.reshape(x.shape[0] // 8, 8, x.shape[1]) * rows[None]).reshape(x.shape)

    pieces = [(k, h) for k in range(K) for h in (0, HALF)]

    def pipeline(prepare, start, chain, finish, end):
        begun, left, n = {}, {}, len(pieces)
        for t in range(-2, n + 1):
            if 0 <= t + 1 < n:
                begun[t + 1] = start(*pieces[t + 1])
            if 0 <= t - 1 < n:
                left[t - 1] = finish(*pieces[t - 1])
            if 0 <= t < n:
                chain(*pieces[t], begun.pop(t))
            if 0 <= t - 1 < n:
                end(*pieces[t - 1], left.pop(t - 1))
            if 0 <= t + 2 < n and prepare is not None:
                prepare(*pieces[t + 2])

    def first_start(k, h):
        return dot(w1t[...], given[k, :, h : h + HALF])

    def first_chain(k, h, v):
        for c in range(0, LAT, ROWS):
            part = v[c : c + ROWS]
            t = jnp.tanh(part)
            vt = part * t
            latent[k, c : c + ROWS, h : h + HALF] = (part + vt).astype(BF16)
            slope1[k, c : c + ROWS, h : h + HALF] = ((1.0 + t) * ((1.0 + part) - vt)).astype(BF16)

    def first_mix(k, h):
        return dot(wct[...], latent[k, :, h : h + HALF])

    def first_end(k, h, made):
        mix0[k, :, h : h + HALF] = made[0:C]
        mix[k, :, h : h + HALF] = by_row(made[0:C], wide_env[k, :, h : h + HALF])
        gain1[k, :, h : h + HALF] = made[C : C + 8]

    for k in range(K):
        basis = jnp.exp(-rates * sq[k : k + 1, :]) * env[k : k + 1, :]
        codes = jnp.where(row8 < 2, centre_code, ncode[k : k + 1, :])
        hot = jnp.where(jnp.logical_and(codes == kind, row8 < 4), 1.0, 0.0)
        given[k] = jnp.concatenate([basis, hot], axis=0).astype(BF16)
    pipeline(None, first_start, first_chain, first_mix, first_end)

    def weigh(parts, source_of, out):
        for j in range(0, ATOMS, BA):
            for c in range(0, C, STRIP):
                total = [None] * 9
                for k in range(K):
                    read = [source_of(k, l, c, j) for l in range(parts)]
                    for m in range(9):
                        term = read[DEGREE[m] if parts == 3 else 0]
                        if m:
                            term = by_row(term, harm[m - 1, k, :, j : j + BA])
                        total[m] = term if k == 0 else total[m] + term
                for m in range(9):
                    out[m, c : c + STRIP, j : j + BA] = total[m] * NORM

    weigh(1, lambda k, l, c, j: mix[k, c : c + STRIP, j : j + BA], dens)

    def second_in(k, j):
        h = [None] + [harm[m, k, :, j : j + BA] for m in range(8)]
        mixed = mix[k, :, j : j + BA]
        for l, terms in enumerate(([0], [1, 2, 3], [4, 5, 6, 7, 8])):
            prod = None
            for m in terms:
                term = dens[m, :, j : j + BA]
                if m:
                    term = by_row(term, h[m])
                prod = term if prod is None else prod + term
            prods[k, l * C : l * C + C, j : j + BA] = prod
            scal[k, l * C : l * C + C, j : j + BA] = (prod * mixed).astype(BF16)

    def second_prepare(k, h):
        second_in(k, h)
        second_in(k, h + BA)

    def second_start(k, h):
        return dot(wut[...], scal[k, :, h : h + HALF])

    def second_chain(k, h, v):
        gains = [0.0] * (HALF // BA)
        for c in range(0, LAT, ROWS):
            part = v[c : c + ROWS]
            t = jnp.tanh(part)
            vt = part * t
            updated = part + vt
            slope2[k, c : c + ROWS, h : h + HALF] = ((1.0 + t) * ((1.0 + part) - vt)).astype(BF16)
            weight = ew_wide[c : c + ROWS, :]
            for j in range(HALF // BA):
                gain = updated[:, j * BA : j * BA + BA] * weight
                gains[j] = gains[j] + fold(gain)
        for j in range(HALF // BA):
            gain2[k, :, h + j * BA : h + j * BA + BA] = gains[j]

    def second_back(k, h):
        return dot(wue[...], slope2[k, :, h : h + HALF])

    def second_end(k, h, back):
        for j in range(0, HALF, BA):
            at_j = slice(h + j, h + j + BA)
            env_j = wide_env[k, :, at_j]
            both = by_row(mix[k, :, at_j], env_j)
            partial = None
            for l in range(3):
                flow = back[l * C : l * C + C, j : j + BA]
                term = flow * prods[k, l * C : l * C + C, at_j]
                partial = term if partial is None else partial + term
                dscal[k, l * C : l * C + C, at_j] = flow * both
            dmix[k, :, at_j] = by_row(partial, env_j)

    pipeline(second_prepare, second_start, second_chain, second_back, second_end)

    weigh(3, lambda k, l, c, j: dscal[k, l * C + c : l * C + c + STRIP, j : j + BA], ddens)

    row_in = lax.broadcasted_iota(jnp.int32, (4 * K, 8, BA), 1)
    masks = [row_in < 4, (row_in & 2) == 0, (row_in & 1) == 0]

    def rows_of(parts):
        pairs = [
            jnp.where(masks[0], parts[i], parts[i + 4])
            + pltpu.roll(jnp.where(masks[0], parts[i + 4], parts[i]), 4, 1)
            for i in range(4)
        ]
        for size in (2, 1):
            pairs = [
                jnp.where(
                    masks[3 - size],
                    pairs[i] + pltpu.roll(pairs[i], 8 - size, 1),
                    pairs[i + size] + pltpu.roll(pairs[i + size], size, 1),
                )
                for i in range(size)
            ]
        return pairs[0]

    def third_in(k, j):
        at_j = slice(j, j + BA)
        parts = [0.0] * 8
        pull = 0.0
        for c in range(0, C, BITE):
            at_c = slice(c, c + BITE)
            mixed = mix[k, at_c, at_j]
            flows = [dscal[k, l * C + c : l * C + c + BITE, at_j] for l in range(3)]
            total = dmix[k, at_c, at_j] + ddens[0, at_c, at_j]
            for m in range(1, 9):
                slope = ddens[m, at_c, at_j]
                total = total + by_row(slope, harm[m - 1, k, :, at_j])
                parts[m - 1] = parts[m - 1] + fold(mixed * slope + flows[DEGREE[m]] * dens[m, at_c, at_j])
            pull = pull + fold(total * mix0[k, at_c, at_j])
            dlow[k, at_c, at_j] = by_row(total, wide_env[k, :, at_j]).astype(BF16)
        for m in range(8):
            folded[m, K * (j // BA) + k] = parts[m]
        gain3[k, :, at_j] = pull

    def third_prepare(k, h):
        third_in(k, h)
        third_in(k, h + BA)

    def third_start(k, h):
        return dot(wcc[...], dlow[k, :, h : h + HALF])

    def third_chain(k, h, d):
        for c in range(0, LAT, ROWS):
            part = d[c : c + ROWS] * slope1[k, c : c + ROWS, h : h + HALF].astype(F32)
            dpre[k, c : c + ROWS, h : h + HALF] = part.astype(BF16)

    def third_back(k, h):
        return dot(w1[...], dpre[k, :, h : h + HALF])

    def third_end(k, h, db):
        db = db[0:8] * jnp.exp(-rates[:, h : h + HALF] * edge[0, k : k + 1, h : h + HALF])
        dbasis[k, :, h : h + HALF] = db

    row16 = lax.broadcasted_iota(jnp.int32, (16, ATOMS), 0)
    for k in range(K):
        env_k = env[k : k + 1, :]
        high = env_k.astype(BF16).astype(F32)
        tail = jnp.where(row16 == 0, high, jnp.where(row16 == 1, env_k - high, 0.0))
        dlow[k, C : C + 16, :] = tail.astype(BF16)
    pipeline(third_prepare, third_start, third_chain, third_back, third_end)

    turned_rows = rows_of([folded[m] for m in range(8)]).reshape(ATOMS // BA, 8 * K, BA)
    dharm[...] = turned_rows
    top = lax.broadcasted_iota(jnp.int32, (K, 8, ATOMS), 1) == 0
    sums = jnp.sum(gain2[...] + jnp.where(top, gain1[...], 0.0), axis=1)
    back_rows = dbasis[...]
    pulled = jnp.sum(gain3[...] + back_rows, axis=1)
    shrunk = jnp.sum(back_rows * rates[None], axis=1)
    result[12, :, :] = jnp.sum(sums * env, axis=0, keepdims=True)
    denv = sums + pulled
    dsq = -shrunk * env + denv * live * cut * (-2.0 / 64.0)
    dh = [None] + [
        jnp.concatenate([dharm[j, pl.ds(m, K, stride=8), :] for j in range(ATOMS // BA)], axis=1)
        for m in range(8)
    ]
    gx = SCALE * (dh[1] + ROOT3 * (uy * dh[4] + uz * dh[7] + ux * dh[8]) - ux * dh[6]) + 2.0 * rx * dsq
    gy = SCALE * (dh[2] + ROOT3 * (ux * dh[4] + uz * dh[5] - uy * dh[8]) - uy * dh[6]) + 2.0 * ry * dsq
    gz = SCALE * (dh[3] + ROOT3 * (uy * dh[5] + ux * dh[7]) + 2.0 * uz * dh[6]) + 2.0 * rz * dsq
    grads = (gx, gy, gz)
    terms = [r * g for r in (rx, ry, rz) for g in grads] + list(grads)
    for v, term in enumerate(terms):
        for j in range(ATOMS // BA):
            vals[j, 8 * v : 8 * v + 8, :] = term[:, j * BA : j * BA + BA]
    vals[:, 96:128, :] = jnp.zeros((ATOMS // BA, 32, BA), F32)

    for k in range(K):
        group = jnp.broadcast_to(lax.shift_right_logical(nbr_v[0, 0, k : k + 1, :], 8), (8, ATOMS))
        term = jnp.concatenate(
            [vals[j, pl.ds(k, 16, stride=8), :] for j in range(ATOMS // BA)], axis=1
        )
        upper = term[0:8]
        lower = term[8:16] + pltpu.roll(term[8:16], 4, 0)
        later = group - jnp.where(row8 < 4, 0, 1)
        pieces = [jnp.where(group == g, upper, 0.0) for g in range(GROUPS)]
        pieces += [jnp.where(later == g, lower, 0.0) for g in range(0, GROUPS, 2)]
        spread = jnp.concatenate(pieces, axis=0).astype(BF16)
        found = dot(spread, turned_hot[k])
        first_part = found[0:144].reshape(9, 16, SPAN)
        second_part = found[144:216].reshape(9, 8, SPAN)
        if k == 0:
            ghost[:, 0:16, :] = first_part
            ghost[:, 16:24, :] = second_part
        else:
            ghost[:, 0:16, :] += first_part
            ghost[:, 16:24, :] += second_part

    outs = []
    for slot, (dr, dc) in enumerate(NEAR):
        copy = pltpu.make_async_remote_copy(
            src_ref=ghost.at[(dr + 1) * 3 + dc + 1],
            dst_ref=ghost_in.at[slot],
            send_sem=send_out.at[slot],
            recv_sem=recv_out.at[slot],
            device_id=at(dr, dc),
            device_id_type=MESH,
        )
        copy.start()
        outs.append(copy)
    own_sums = jnp.concatenate([jnp.sum(t, axis=0, keepdims=True) for t in terms], axis=0)
    total = ghost[4]
    for slot, copy in enumerate(outs):
        copy.wait_recv()
        total = total + ghost_in[slot]
    total = jnp.concatenate(
        [
            jnp.concatenate([total[0:8], total[16:20]], axis=0),
            jnp.concatenate([total[8:16], total[20:24]], axis=0),
        ],
        axis=1,
    )
    total = jnp.where(
        lax.broadcasted_iota(jnp.int32, (12, ATOMS), 0) < 9,
        -0.5 * (own_sums + total),
        own_sums - total,
    )
    for v in range(12):
        result[v, :, :] = total[v : v + 1]
    for copy in sends + outs:
        copy.wait_send()


def share_out(result, forces, virial, energies):
    virial[...] = result[0:9]
    forces[...] = result[9:12]
    energies[...] = result[12:13]


def solution(mesh):
    n_row, n_col = mesh.shape["row"], mesh.shape["col"]
    hbm = pl.BlockSpec(memory_space=pltpu.HBM)

    def on_device(pos, spc, valid, rcount, ccount, nbr, rate, rw, ct, nt, cw, uw, ew):
        args = (pos.transpose(0, 2, 1, 3), spc, valid, rcount, ccount, nbr, rate, rw, ct, nt, cw.T, uw, ew)
        held = [pltpu.VMEM(a.shape, a.dtype) for a in args]
        held[6] = pltpu.SMEM(rate.shape, rate.dtype)
        result = pl.pallas_call(
            functools.partial(kernel, n_row, n_col),
            out_shape=jax.ShapeDtypeStruct((13, 1, ATOMS), F32),
            in_specs=[hbm] * len(args),
            out_specs=pl.BlockSpec(memory_space=pltpu.VMEM),
            scratch_shapes=held
            + [
                pltpu.SemaphoreType.DMA((13,)),
                pltpu.VMEM((8, BA), F32),
                pltpu.VMEM((len(REACH), 8, BA), F32),
                pltpu.VMEM((144, SPAN), F32),
                pltpu.VMEM((144, SPAN), BF16),
                pltpu.VMEM((ATOMS // BA, 8 * K, BA), F32),
                pltpu.VMEM((K, SPAN, ATOMS), BF16),
                pltpu.VMEM((K, ATOMS, SPAN), BF16),
                pltpu.VMEM((8, K, 8, ATOMS), F32),
                pltpu.VMEM((8, K, ATOMS), F32),
                pltpu.VMEM((K, 8, ATOMS), F32),
                pltpu.VMEM((128, LAT), F32),
                pltpu.VMEM((LAT, 16), BF16),
                pltpu.VMEM((16, LAT), BF16),
                pltpu.VMEM((LAT, 3 * C), BF16),
                pltpu.VMEM((3 * C, LAT), BF16),
                pltpu.VMEM((80, LAT), BF16),
                pltpu.VMEM((LAT, 80), BF16),
                pltpu.VMEM((LAT, BA), F32),
                pltpu.VMEM((K, 16, ATOMS), BF16),
                pltpu.VMEM((K, LAT, ATOMS), BF16),
                pltpu.VMEM((K, LAT, ATOMS), BF16),
                pltpu.VMEM((K, LAT, ATOMS), BF16),
                pltpu.VMEM((K, C, ATOMS), F32),
                pltpu.VMEM((K, C, ATOMS), F32),
                pltpu.VMEM((9, C, ATOMS), F32),
                pltpu.VMEM((9, C, ATOMS), F32),
                pltpu.VMEM((K, 3 * C, ATOMS), F32),
                pltpu.VMEM((K, 3 * C, ATOMS), BF16),
                pltpu.VMEM((K, 3 * C, ATOMS), F32),
                pltpu.VMEM((K, C, ATOMS), F32),
                pltpu.VMEM((ATOMS // BA, 8 * K, BA), F32),
                pltpu.VMEM((8, 4 * K, 8, BA), F32),
                pltpu.VMEM((K, 8, ATOMS), F32),
                pltpu.VMEM((K, 8, ATOMS), F32),
                pltpu.VMEM((K, 8, ATOMS), F32),
                pltpu.VMEM((K, 8, ATOMS), F32),
                pltpu.VMEM((K, 80, ATOMS), BF16),
                pltpu.VMEM((K, LAT, ATOMS), BF16),
                pltpu.VMEM((ATOMS // BA, 128, BA), F32),
                pltpu.VMEM((9, 24, SPAN), F32),
                pltpu.VMEM((8, 24, SPAN), F32),
                pltpu.SemaphoreType.DMA((len(REACH),)),
                pltpu.SemaphoreType.DMA((len(REACH),)),
                pltpu.SemaphoreType.DMA((len(NEAR),)),
                pltpu.SemaphoreType.DMA((len(NEAR),)),
            ],
            compiler_params=pltpu.CompilerParams(
                collective_id=0, has_side_effects=True, vmem_limit_bytes=64 * 1024 * 1024
            ),
        )(*args)
        forces, virial, energies = pl.pallas_call(
            share_out,
            out_shape=[jax.ShapeDtypeStruct((n, 1, ATOMS), F32) for n in (3, 9, 1)],
            in_specs=[pl.BlockSpec(memory_space=pltpu.VMEM)],
            out_specs=[pl.BlockSpec(memory_space=pltpu.VMEM)] * 3,
            compiler_params=pltpu.CompilerParams(vmem_limit_bytes=1 << 20),
        )(result)
        return (
            forces.reshape(1, 3, 1, ATOMS).transpose(0, 2, 1, 3),
            virial.reshape(1, 9, 1, ATOMS).transpose(0, 2, 1, 3),
            energies,
        )

    in_specs = (
        P("row", "col", None, None),
        P("row", "col", None),
        P("row", "col", None),
        P("row", "col"),
        P("row", "col"),
        P("row", "col", None, None),
    ) + (P(),) * 7
    out_specs = (P("row", "col", None, None), P("row", "col", None, None), P("row", "col", None))
    return jax.shard_map(on_device, mesh=mesh, in_specs=in_specs, out_specs=out_specs, check_vma=False)
```

```python
import functools
import math

import jax
import jax.numpy as jnp
from jax import lax
from jax.experimental import pallas as pl
from jax.experimental.pallas import tpu as pltpu
from jax.sharding import PartitionSpec as P

K = 8
BA = 128
C = 64
LAT = 512
ATOMS = 512
SPAN = 256
GROUPS = 18
SLAB = 8.0
SCALE = 0.25
ROOT3 = math.sqrt(3.0)
NORM = 1.0 / math.sqrt(8.0)
F32 = jnp.float32
BF16 = jnp.bfloat16
MESH = pl.DeviceIdType.MESH

NEAR = [(a, b) for a in (-1, 0, 1) for b in (-1, 0, 1) if (a, b) != (0, 0)]
REACH = NEAR + [(2, b) for b in (-1, 0, 1)] + [(a, 2) for a in (-1, 0, 1)]
DEGREE = [0, 1, 1, 1, 2, 2, 2, 2, 2]
HALF = 256
PARTS = ((0, 2, 6, 8, 3, 5), (1, 7, 4))
STRIP = 16
ROWS = 64
BITE = 32


def dot(a, b):
    return lax.dot_general(a, b, (((1,), (0,)), ((), ())), preferred_element_type=F32)


def kernel(
    n_row,
    n_col,
    pos,
    spc,
    valid,
    rcount,
    ccount,
    nbr,
    rate,
    rw,
    ct,
    nt,
    cw,
    uw,
    ew,
    result,
    pos_v,
    spc_v,
    valid_v,
    rcount_v,
    ccount_v,
    nbr_v,
    rate_v,
    rw_v,
    ct_v,
    nt_v,
    cw_v,
    uw_v,
    ew_v,
    load_sem,
    own,
    inbox,
    near_stage,
    near_table,
    rel_code,
    onehot,
    turned_hot,
    harm,
    edge,
    wide_env,
    w_stage,
    w1t,
    w1,
    wut,
    wue,
    wct,
    wcc,
    ew_wide,
    given,
    latent,
    slope1,
    slope2,
    mix0,
    mix,
    dens,
    ddens,
    prods,
    scal,
    dscal,
    dmix,
    dharm,
    folded,
    gain1,
    gain2,
    gain3,
    dbasis,
    dlow,
    dpre,
    vals,
    ghost,
    ghost_in,
    send_in,
    recv_in,
    send_out,
    recv_out,
):
    row = lax.axis_index("row")
    col = lax.axis_index("col")

    def at(dr, dc):
        return (lax.rem(row + (dr + n_row), n_row), lax.rem(col + (dc + n_col), n_col))

    loads = [
        pltpu.make_async_copy(there, here, load_sem.at[i])
        for i, (there, here) in enumerate(
            [
                (pos, pos_v),
                (spc, spc_v),
                (valid, valid_v),
                (rcount, rcount_v),
                (ccount, ccount_v),
                (nbr, nbr_v),
                (rate, rate_v),
                (rw, rw_v),
                (ct, ct_v),
                (nt, nt_v),
                (cw, cw_v),
                (uw, uw_v),
                (ew, ew_v),
            ]
        )
    ]
    for load in loads[:5]:
        load.start()
    barrier = pltpu.get_barrier_semaphore()
    for dr, dc in REACH:
        pl.semaphore_signal(barrier, inc=1, device_id=at(-dr, -dc), device_id_type=MESH)
    for load in loads[5:]:
        load.start()
    for load in loads[:5]:
        load.wait()

    code = (valid_v[0] * (spc_v[0] + 1)).astype(F32)
    moves = jnp.concatenate(
        [
            jnp.where(jnp.broadcast_to(ccount_v[...], (1, BA)) > 0, 1.0, 0.0),
            jnp.where(jnp.broadcast_to(rcount_v[...], (1, BA)) > 0, 1.0, 0.0),
        ],
        axis=1,
    )
    code = code * (1.0 - 2.0 * moves)
    for half in range(2):
        at_half = slice(half * BA, half * BA + BA)
        for i in range(3):
            own[4 * half + i : 4 * half + i + 1, :] = pos_v[0, i][:, at_half]
        own[4 * half + 3 : 4 * half + 4, :] = code[:, at_half]
    pl.semaphore_wait(barrier, len(REACH))
    sends = []
    for slot, (dr, dc) in enumerate(REACH):
        copy = pltpu.make_async_remote_copy(
            src_ref=own,
            dst_ref=inbox.at[slot],
            send_sem=send_in.at[slot],
            recv_sem=recv_in.at[slot],
            device_id=at(dr, dc),
            device_id_type=MESH,
        )
        copy.start()
        sends.append(copy)

    for load in loads[5:]:
        load.wait()
    w_stage[...] = jnp.zeros_like(w_stage)
    w_stage[0:8, :] = rw_v[...].astype(F32) * 0.5
    w_stage[8:10, :] = ct_v[...].astype(F32) * 0.5
    w_stage[10:12, :] = nt_v[...].astype(F32) * 0.5
    w1[...] = w_stage[0:16, :].astype(BF16)
    w1t[...] = w_stage[...].T[:, 0:16].astype(BF16)
    half_u = uw_v[...].astype(F32) * 0.5
    ew_row = ew_v[...].astype(F32).reshape(1, LAT)
    wue[...] = (half_u * ew_row).astype(BF16)
    wut[...] = half_u.T.astype(BF16)
    w_stage[0:C, :] = cw_v[...].astype(F32)
    w_stage[C : C + 1, :] = ew_row
    w_stage[C + 1 : C + 2, :] = ew_row
    wct[...] = w_stage[0:80, :].astype(BF16)
    turned = w_stage[...].T
    wcc[...] = turned[:, 0:80].astype(BF16)
    ew_wide[...] = jnp.broadcast_to(turned[:, C : C + 1], (LAT, BA))

    place_of = lax.broadcasted_iota(jnp.int32, (SPAN, ATOMS), 0)

    for k in range(K):
        place = nbr_v[0, 0, k : k + 1, :] & (SPAN - 1)
        marks = jnp.where(place_of == place, 1.0, 0.0)
        onehot[k] = marks.astype(BF16)
        turned_hot[k] = marks.T.astype(BF16)

    for copy in sends:
        copy.wait_recv()

    row_of = lax.broadcasted_iota(jnp.int32, (8, BA), 0)

    def source(dr, dc):
        if (dr, dc) == (0, 0):
            return own
        return inbox.at[REACH.index((-dr, -dc))]

    centre = None
    for p in range(9):
        a, b = p // 3 - 1, p % 3 - 1
        here = source(a, b)[...]
        tiles = []
        for tile, dx, dy in (
            (pltpu.roll(jnp.where(row_of < 4, here, source(a - 1, b)[...]), 4, 0), -SLAB, 0.0),
            (jnp.where(row_of < 4, source(a, b - 1)[...], here), 0.0, -SLAB),
        ):
            tile = jnp.where(row_of == 3, jnp.maximum(-tile, 0.0), tile)
            tile = jnp.where(row_of == 7, jnp.maximum(tile, 0.0), tile)
            shift = jnp.where(row_of == 4, SLAB * a, jnp.where(row_of == 5, SLAB * b, 0.0))
            shift = jnp.where(row_of == 0, SLAB * a + dx, jnp.where(row_of == 1, SLAB * b + dy, shift))
            tiles.append(tile + shift)
        tile = jnp.concatenate(tiles, axis=1)
        high = tile.astype(BF16).astype(F32)
        near_stage[8 * p : 8 * p + 8, :] = high
        near_stage[72 + 8 * p : 80 + 8 * p, :] = tile - high
        if p == 4:
            centre = jnp.concatenate([tile, pltpu.roll(tile, 4, 0)], axis=1)
    near_table[...] = near_stage[...].astype(BF16)
    row8 = lax.broadcasted_iota(jnp.int32, (8, ATOMS), 0)
    centre_xyz = jnp.where(row8 < 3, centre, 0.0)
    centre_code = centre[3:4, :]

    for k in range(K):
        index = jnp.broadcast_to(nbr_v[0, 0, k : k + 1, :], (8, ATOMS))
        block = lax.shift_right_logical(index, 9)
        found = dot(near_table[...], onehot[k])
        picked = found[0:8] + found[72:80]
        for p in range(1, 9):
            picked = jnp.where(block == p, found[8 * p : 8 * p + 8] + found[72 + 8 * p : 80 + 8 * p], picked)
        picked = jnp.where((index & SPAN) != 0, pltpu.roll(picked, 4, 0), picked) - centre_xyz
        for j in range(ATOMS // BA):
            rel_code[j, 8 * k : 8 * k + 8, :] = picked[:, j * BA : j * BA + BA]

    rx, ry, rz, ncode = [
        jnp.concatenate([rel_code[j, pl.ds(c, K, stride=8), :] for j in range(ATOMS // BA)], axis=1)
        for c in range(4)
    ]
    live = jnp.where(jnp.logical_and(ncode > 0.5, centre_code > 0.5), 1.0, 0.0)
    sq = rx * rx + ry * ry + rz * rz
    cut = jnp.maximum(1.0 - sq * (1.0 / 64.0), 0.0)
    env = cut * cut * live
    ux, uy, uz = rx * SCALE, ry * SCALE, rz * SCALE
    norm = ux * ux + uy * uy + uz * uz
    for m, h in enumerate(
        [
            ux,
            uy,
            uz,
            ROOT3 * ux * uy,
            ROOT3 * uy * uz,
            0.5 * (3.0 * uz * uz - norm),
            ROOT3 * ux * uz,
            0.5 * ROOT3 * (ux * ux - uy * uy),
        ]
    ):
        for k in range(K):
            harm[m, k] = jnp.broadcast_to(h[k : k + 1, :], (8, ATOMS))
    for k in range(K):
        wide_env[k] = jnp.broadcast_to(env[k : k + 1, :], (8, ATOMS))
    edge[0] = sq
    edge[1] = env
    edge[2] = ncode

    rates = jnp.zeros((8, ATOMS), F32)
    for n in range(8):
        rates = jnp.where(row8 == n, rate_v[n], rates)
    kind = jnp.where(row8 % 2 == 0, 1.0, 2.0)

    def fold(x):
        return jnp.sum(x.reshape(x.shape[0] // 8, 8, BA), axis=0)

    def by_row(x, rows):
        return (x.reshape(x.shape[0] // 8, 8, x.shape[1]) * rows[None]).reshape(x.shape)

    pieces = [(k, h) for k in range(K) for h in (0, HALF)]

    def pipeline(prepare, start, chain, finish, end):
        begun, left, n = {}, {}, len(pieces)
        for t in range(-2, n + 1):
            if 0 <= t + 1 < n:
                begun[t + 1] = start(*pieces[t + 1])
            if 0 <= t - 1 < n:
                left[t - 1] = finish(*pieces[t - 1])
            if 0 <= t < n:
                chain(*pieces[t], begun.pop(t))
            if 0 <= t - 1 < n:
                end(*pieces[t - 1], left.pop(t - 1))
            if 0 <= t + 2 < n and prepare is not None:
                prepare(*pieces[t + 2])

    def first_start(k, h):
        return dot(w1t[...], given[k, :, h : h + HALF])

    def first_chain(k, h, v):
        for c in range(0, LAT, ROWS):
            part = v[c : c + ROWS]
            t = jnp.tanh(part)
            vt = part * t
            latent[k, c : c + ROWS, h : h + HALF] = (part + vt).astype(BF16)
            slope1[k, c : c + ROWS, h : h + HALF] = ((1.0 + t) * ((1.0 + part) - vt)).astype(BF16)

    def first_mix(k, h):
        return dot(wct[...], latent[k, :, h : h + HALF])

    def first_end(k, h, made):
        mix0[k, :, h : h + HALF] = made[0:C]
        mix[k, :, h : h + HALF] = by_row(made[0:C], wide_env[k, :, h : h + HALF])
        gain1[k, :, h : h + HALF] = made[C : C + 8]

    for k in range(K):
        basis = jnp.exp(-rates * sq[k : k + 1, :]) * env[k : k + 1, :]
        codes = jnp.where(row8 < 2, centre_code, ncode[k : k + 1, :])
        hot = jnp.where(jnp.logical_and(codes == kind, row8 < 4), 1.0, 0.0)
        given[k] = jnp.concatenate([basis, hot], axis=0).astype(BF16)
    pipeline(None, first_start, first_chain, first_mix, first_end)

    def weigh(parts, source_of, out):
        for j in range(0, ATOMS, BA):
            for c in range(0, C, STRIP):
                total = [None] * 9
                for k in range(K):
                    read = [source_of(k, l, c, j) for l in range(parts)]
                    for m in range(9):
                        term = read[DEGREE[m] if parts == 3 else 0]
                        if m:
                            term = by_row(term, harm[m - 1, k, :, j : j + BA])
                        total[m] = term if k == 0 else total[m] + term
                for m in range(9):
                    out[m, c : c + STRIP, j : j + BA] = total[m] * NORM

    weigh(1, lambda k, l, c, j: mix[k, c : c + STRIP, j : j + BA], dens)

    def second_in(k, j):
        h = [None] + [harm[m, k, :, j : j + BA] for m in range(8)]
        mixed = mix[k, :, j : j + BA]
        for l, terms in enumerate(([0], [1, 2, 3], [4, 5, 6, 7, 8])):
            prod = None
            for m in terms:
                term = dens[m, :, j : j + BA]
                if m:
                    term = by_row(term, h[m])
                prod = term if prod is None else prod + term
            prods[k, l * C : l * C + C, j : j + BA] = prod
            scal[k, l * C : l * C + C, j : j + BA] = (prod * mixed).astype(BF16)

    def second_prepare(k, h):
        second_in(k, h)
        second_in(k, h + BA)

    def second_start(k, h):
        return dot(wut[...], scal[k, :, h : h + HALF])

    def second_chain(k, h, v):
        gains = [0.0] * (HALF // BA)
        for c in range(0, LAT, ROWS):
            part = v[c : c + ROWS]
            t = jnp.tanh(part)
            vt = part * t
            updated = part + vt
            slope2[k, c : c + ROWS, h : h + HALF] = ((1.0 + t) * ((1.0 + part) - vt)).astype(BF16)
            weight = ew_wide[c : c + ROWS, :]
            for j in range(HALF // BA):
                gain = updated[:, j * BA : j * BA + BA] * weight
                gains[j] = gains[j] + fold(gain)
        for j in range(HALF // BA):
            gain2[k, :, h + j * BA : h + j * BA + BA] = gains[j]

    def second_back(k, h):
        return dot(wue[...], slope2[k, :, h : h + HALF])

    def second_end(k, h, back):
        for j in range(0, HALF, BA):
            at_j = slice(h + j, h + j + BA)
            env_j = wide_env[k, :, at_j]
            both = by_row(mix[k, :, at_j], env_j)
            partial = None
            for l in range(3):
                flow = back[l * C : l * C + C, j : j + BA]
                term = flow * prods[k, l * C : l * C + C, at_j]
                partial = term if partial is None else partial + term
                dscal[k, l * C : l * C + C, at_j] = flow * both
            dmix[k, :, at_j] = by_row(partial, env_j)

    pipeline(second_prepare, second_start, second_chain, second_back, second_end)

    weigh(3, lambda k, l, c, j: dscal[k, l * C + c : l * C + c + STRIP, j : j + BA], ddens)

    row_in = lax.broadcasted_iota(jnp.int32, (4 * K, 8, BA), 1)
    masks = [row_in < 4, (row_in & 2) == 0, (row_in & 1) == 0]

    def rows_of(parts):
        pairs = [
            jnp.where(masks[0], parts[i], parts[i + 4])
            + pltpu.roll(jnp.where(masks[0], parts[i + 4], parts[i]), 4, 1)
            for i in range(4)
        ]
        for size in (2, 1):
            pairs = [
                jnp.where(
                    masks[3 - size],
                    pairs[i] + pltpu.roll(pairs[i], 8 - size, 1),
                    pairs[i + size] + pltpu.roll(pairs[i + size], size, 1),
                )
                for i in range(size)
            ]
        return pairs[0]

    def third_in(k, j):
        at_j = slice(j, j + BA)
        parts = [0.0] * 8
        pull = 0.0
        for c in range(0, C, BITE):
            at_c = slice(c, c + BITE)
            mixed = mix[k, at_c, at_j]
            flows = [dscal[k, l * C + c : l * C + c + BITE, at_j] for l in range(3)]
            total = dmix[k, at_c, at_j] + ddens[0, at_c, at_j]
            for m in range(1, 9):
                slope = ddens[m, at_c, at_j]
                total = total + by_row(slope, harm[m - 1, k, :, at_j])
                parts[m - 1] = parts[m - 1] + fold(mixed * slope + flows[DEGREE[m]] * dens[m, at_c, at_j])
            pull = pull + fold(total * mix0[k, at_c, at_j])
            dlow[k, at_c, at_j] = by_row(total, wide_env[k, :, at_j]).astype(BF16)
        for m in range(8):
            folded[m, K * (j // BA) + k] = parts[m]
        gain3[k, :, at_j] = pull

    def third_prepare(k, h):
        third_in(k, h)
        third_in(k, h + BA)

    def third_start(k, h):
        return dot(wcc[...], dlow[k, :, h : h + HALF])

    def third_chain(k, h, d):
        for c in range(0, LAT, ROWS):
            part = d[c : c + ROWS] * slope1[k, c : c + ROWS, h : h + HALF].astype(F32)
            dpre[k, c : c + ROWS, h : h + HALF] = part.astype(BF16)

    def third_back(k, h):
        return dot(w1[...], dpre[k, :, h : h + HALF])

    def third_end(k, h, db):
        db = db[0:8] * jnp.exp(-rates[:, h : h + HALF] * edge[0, k : k + 1, h : h + HALF])
        dbasis[k, :, h : h + HALF] = db

    row16 = lax.broadcasted_iota(jnp.int32, (16, ATOMS), 0)
    for k in range(K):
        env_k = env[k : k + 1, :]
        high = env_k.astype(BF16).astype(F32)
        tail = jnp.where(row16 == 0, high, jnp.where(row16 == 1, env_k - high, 0.0))
        dlow[k, C : C + 16, :] = tail.astype(BF16)
    pipeline(third_prepare, third_start, third_chain, third_back, third_end)

    turned_rows = rows_of([folded[m] for m in range(8)]).reshape(ATOMS // BA, 8 * K, BA)
    dharm[...] = turned_rows
    top = lax.broadcasted_iota(jnp.int32, (K, 8, ATOMS), 1) == 0
    sums = jnp.sum(gain2[...] + jnp.where(top, gain1[...], 0.0), axis=1)
    back_rows = dbasis[...]
    pulled = jnp.sum(gain3[...] + back_rows, axis=1)
    shrunk = jnp.sum(back_rows * rates[None], axis=1)
    result[12, :, :] = jnp.sum(sums * env, axis=0, keepdims=True)
    denv = sums + pulled
    dsq = -shrunk * env + denv * live * cut * (-2.0 / 64.0)
    dh = [None] + [
        jnp.concatenate([dharm[j, pl.ds(m, K, stride=8), :] for j in range(ATOMS // BA)], axis=1)
        for m in range(8)
    ]
    gx = SCALE * (dh[1] + ROOT3 * (uy * dh[4] + uz * dh[7] + ux * dh[8]) - ux * dh[6]) + 2.0 * rx * dsq
    gy = SCALE * (dh[2] + ROOT3 * (ux * dh[4] + uz * dh[5] - uy * dh[8]) - uy * dh[6]) + 2.0 * ry * dsq
    gz = SCALE * (dh[3] + ROOT3 * (uy * dh[5] + ux * dh[7]) + 2.0 * uz * dh[6]) + 2.0 * rz * dsq
    grads = (gx, gy, gz)
    terms = [r * g for r in (rx, ry, rz) for g in grads] + list(grads)
    for v, term in enumerate(terms):
        for j in range(ATOMS // BA):
            vals[j, 8 * v : 8 * v + 8, :] = term[:, j * BA : j * BA + BA]
    vals[:, 96:128, :] = jnp.zeros((ATOMS // BA, 32, BA), F32)

    def scatter(blocks):
        for k in range(K):
            group = jnp.broadcast_to(lax.shift_right_logical(nbr_v[0, 0, k : k + 1, :], 8), (8, ATOMS))
            term = jnp.concatenate(
                [vals[j, pl.ds(k, 16, stride=8), :] for j in range(ATOMS // BA)], axis=1
            )
            upper = term[0:8]
            lower = term[8:16] + pltpu.roll(term[8:16], 4, 0)
            later = group - jnp.where(row8 < 4, 0, 1)
            pieces = []
            for b in blocks:
                pieces += [jnp.where(group == 2 * b, upper, 0.0), jnp.where(group == 2 * b + 1, upper, 0.0)]
                pieces += [jnp.where(later == 2 * b, lower, 0.0)]
            found = dot(jnp.concatenate(pieces, axis=0).astype(BF16), turned_hot[k])
            for i, b in enumerate(blocks):
                part = found[24 * i : 24 * i + 24]
                ghost[b] = part if k == 0 else ghost[b] + part

    def send(blocks):
        for b in blocks:
            dr, dc = b // 3 - 1, b % 3 - 1
            if (dr, dc) == (0, 0):
                continue
            slot = NEAR.index((dr, dc))
            copy = pltpu.make_async_remote_copy(
                src_ref=ghost.at[b],
                dst_ref=ghost_in.at[slot],
                send_sem=send_out.at[slot],
                recv_sem=recv_out.at[slot],
                device_id=at(dr, dc),
                device_id_type=MESH,
            )
            copy.start()
            outs[slot] = copy

    outs = [None] * len(NEAR)
    for blocks in PARTS:
        scatter(blocks)
        send(blocks)
    own_sums = jnp.concatenate([jnp.sum(t, axis=0, keepdims=True) for t in terms], axis=0)
    total = ghost[4]
    for slot, copy in enumerate(outs):
        copy.wait_recv()
        total = total + ghost_in[slot]
    total = jnp.concatenate(
        [
            jnp.concatenate([total[0:8], total[16:20]], axis=0),
            jnp.concatenate([total[8:16], total[20:24]], axis=0),
        ],
        axis=1,
    )
    total = jnp.where(
        lax.broadcasted_iota(jnp.int32, (12, ATOMS), 0) < 9,
        -0.5 * (own_sums + total),
        own_sums - total,
    )
    for v in range(12):
        result[v, :, :] = total[v : v + 1]
    for copy in sends + outs:
        copy.wait_send()


def share_out(result, forces, virial, energies):
    virial[...] = result[0:9]
    forces[...] = result[9:12]
    energies[...] = result[12:13]


def solution(mesh):
    n_row, n_col = mesh.shape["row"], mesh.shape["col"]
    hbm = pl.BlockSpec(memory_space=pltpu.HBM)

    def on_device(pos, spc, valid, rcount, ccount, nbr, rate, rw, ct, nt, cw, uw, ew):
        args = (pos.transpose(0, 2, 1, 3), spc, valid, rcount, ccount, nbr, rate, rw, ct, nt, cw.T, uw, ew)
        held = [pltpu.VMEM(a.shape, a.dtype) for a in args]
        held[6] = pltpu.SMEM(rate.shape, rate.dtype)
        result = pl.pallas_call(
            functools.partial(kernel, n_row, n_col),
            out_shape=jax.ShapeDtypeStruct((13, 1, ATOMS), F32),
            in_specs=[hbm] * len(args),
            out_specs=pl.BlockSpec(memory_space=pltpu.VMEM),
            scratch_shapes=held
            + [
                pltpu.SemaphoreType.DMA((13,)),
                pltpu.VMEM((8, BA), F32),
                pltpu.VMEM((len(REACH), 8, BA), F32),
                pltpu.VMEM((144, SPAN), F32),
                pltpu.VMEM((144, SPAN), BF16),
                pltpu.VMEM((ATOMS // BA, 8 * K, BA), F32),
                pltpu.VMEM((K, SPAN, ATOMS), BF16),
                pltpu.VMEM((K, ATOMS, SPAN), BF16),
                pltpu.VMEM((8, K, 8, ATOMS), F32),
                pltpu.VMEM((8, K, ATOMS), F32),
                pltpu.VMEM((K, 8, ATOMS), F32),
                pltpu.VMEM((128, LAT), F32),
                pltpu.VMEM((LAT, 16), BF16),
                pltpu.VMEM((16, LAT), BF16),
                pltpu.VMEM((LAT, 3 * C), BF16),
                pltpu.VMEM((3 * C, LAT), BF16),
                pltpu.VMEM((80, LAT), BF16),
                pltpu.VMEM((LAT, 80), BF16),
                pltpu.VMEM((LAT, BA), F32),
                pltpu.VMEM((K, 16, ATOMS), BF16),
                pltpu.VMEM((K, LAT, ATOMS), BF16),
                pltpu.VMEM((K, LAT, ATOMS), BF16),
                pltpu.VMEM((K, LAT, ATOMS), BF16),
                pltpu.VMEM((K, C, ATOMS), F32),
                pltpu.VMEM((K, C, ATOMS), F32),
                pltpu.VMEM((9, C, ATOMS), F32),
                pltpu.VMEM((9, C, ATOMS), F32),
                pltpu.VMEM((K, 3 * C, ATOMS), F32),
                pltpu.VMEM((K, 3 * C, ATOMS), BF16),
                pltpu.VMEM((K, 3 * C, ATOMS), F32),
                pltpu.VMEM((K, C, ATOMS), F32),
                pltpu.VMEM((ATOMS // BA, 8 * K, BA), F32),
                pltpu.VMEM((8, 4 * K, 8, BA), F32),
                pltpu.VMEM((K, 8, ATOMS), F32),
                pltpu.VMEM((K, 8, ATOMS), F32),
                pltpu.VMEM((K, 8, ATOMS), F32),
                pltpu.VMEM((K, 8, ATOMS), F32),
                pltpu.VMEM((K, 80, ATOMS), BF16),
                pltpu.VMEM((K, LAT, ATOMS), BF16),
                pltpu.VMEM((ATOMS // BA, 128, BA), F32),
                pltpu.VMEM((9, 24, SPAN), F32),
                pltpu.VMEM((8, 24, SPAN), F32),
                pltpu.SemaphoreType.DMA((len(REACH),)),
                pltpu.SemaphoreType.DMA((len(REACH),)),
                pltpu.SemaphoreType.DMA((len(NEAR),)),
                pltpu.SemaphoreType.DMA((len(NEAR),)),
            ],
            compiler_params=pltpu.CompilerParams(
                collective_id=0, has_side_effects=True, vmem_limit_bytes=64 * 1024 * 1024
            ),
        )(*args)
        forces, virial, energies = pl.pallas_call(
            share_out,
            out_shape=[jax.ShapeDtypeStruct((n, 1, ATOMS), F32) for n in (3, 9, 1)],
            in_specs=[pl.BlockSpec(memory_space=pltpu.VMEM)],
            out_specs=[pl.BlockSpec(memory_space=pltpu.VMEM)] * 3,
            compiler_params=pltpu.CompilerParams(vmem_limit_bytes=1 << 20),
        )(result)
        return (
            forces.reshape(1, 3, 1, ATOMS).transpose(0, 2, 1, 3),
            virial.reshape(1, 9, 1, ATOMS).transpose(0, 2, 1, 3),
            energies,
        )

    in_specs = (
        P("row", "col", None, None),
        P("row", "col", None),
        P("row", "col", None),
        P("row", "col"),
        P("row", "col"),
        P("row", "col", None, None),
    ) + (P(),) * 7
    out_specs = (P("row", "col", None, None), P("row", "col", None, None), P("row", "col", None))
    return jax.shard_map(on_device, mesh=mesh, in_specs=in_specs, out_specs=out_specs, check_vma=False)
```
